32 devices in a mesh: dp: 4 (over z), seq: 8 (over y, x, core).
Axes of the slice: x: 2, y: 2, z: 4, core: 2. Of those that a mesh axis runs over, the one named last changes fastest.
Arguments:
- hidden_in: bfloat16 [8, 1024, 768], P('dp', 'seq'), may hold values from -6 to 6
- cotangent: bfloat16 [8, 1024, 768], P('dp', 'seq'), may hold values from -6 to 6
- segment_ids: int32 [8, 1024], P('dp', 'seq'), may hold values from 0 to 5, as said below
- query_weight: bfloat16 [768, 768], P(('dp', 'seq')), may hold values from -0.21875 to 0.21875
- key_weight: bfloat16 [768, 768], P(('dp', 'seq')), may hold values from -0.21875 to 0.21875
- value_weight: bfloat16 [768, 768], P(('dp', 'seq')), may hold values from -0.21875 to 0.21875
- out_weight: bfloat16 [768, 768], P(('dp', 'seq')), may hold values from -1.25 to 1.25
- up_weight: bfloat16 [768, 3072], P(('dp', 'seq')), may hold values from -0.21875 to 0.21875
- down_weight: bfloat16 [3072, 768], P(('dp', 'seq')), may hold values from -0.109375 to 0.109375
- query_bias: bfloat16 [768], P(('dp', 'seq')), may hold values from -1.796875 to 1.796875
- value_bias: bfloat16 [768], P(('dp', 'seq')), may hold values from -1.796875 to 1.796875
- out_bias: bfloat16 [768], P(('dp', 'seq')), may hold values from -1.796875 to 1.796875
- up_bias: bfloat16 [3072], P(('dp', 'seq')), may hold values from -1.796875 to 1.796875
- down_bias: bfloat16 [768], P(('dp', 'seq')), may hold values from -1.796875 to 1.796875
- first_gain: bfloat16 [768], P(('dp', 'seq')), may hold values from 0.5 to 1.5
- first_shift: bfloat16 [768], P(('dp', 'seq')), may hold values from -1.796875 to 1.796875
- second_gain: bfloat16 [768], P(('dp', 'seq')), may hold values from 0.5 to 1.5
- second_shift: bfloat16 [768], P(('dp', 'seq')), may hold values from -1.796875 to 1.796875
Outputs:
- hidden_out: bfloat16 [8, 1024, 768], P('dp', 'seq')
- grad_input: float32 [8, 1024, 768], P('dp', 'seq')
- grad_query_weight: float32 [768, 768], P(('dp', 'seq'))
- grad_key_weight: float32 [768, 768], P(('dp', 'seq'))
- grad_value_weight: float32 [768, 768], P(('dp', 'seq'))
- grad_out_weight: float32 [768, 768], P(('dp', 'seq'))
- grad_up_weight: float32 [768, 3072], P(('dp', 'seq'))
- grad_down_weight: float32 [3072, 768], P(('dp', 'seq'))
- grad_query_bias: float32 [768], P(('dp', 'seq'))
- grad_value_bias: float32 [768], P(('dp', 'seq'))
- grad_out_bias: float32 [768], P(('dp', 'seq'))
- grad_up_bias: float32 [3072], P(('dp', 'seq'))
- grad_down_bias: float32 [768], P(('dp', 'seq'))
- grad_first_gain: float32 [768], P(('dp', 'seq'))
- grad_first_shift: float32 [768], P(('dp', 'seq'))
- grad_second_gain: float32 [768], P(('dp', 'seq'))
- grad_second_shift: float32 [768], P(('dp', 'seq'))
The draws below stay inside these ranges and needn't reach their ends.
Inputs may be any that keep to these rules, and one draw needn't show every extreme that they name: `segment_ids`: ids start at 0 in each sequence and never fall along it. In each group of 2 sequences of one index of dp, one sequence, drawn from the seed, is a single document; in the first group another sequence holds documents of exactly 200 tokens; the others hold documents of 200 to 2000 tokens; the last document of a sequence may be shorter.
All inputs are finite; a program needn't handle non-finite values.
Results may differ from the reference program's by a relative error of at most 0.017.
Values may be sent and summed in bfloat16 or wider, within the bound.
No kernel may reach another device: no remote copies, remote signals or barrier semaphores. Data moves between devices by JAX's collectives and lax.ppermute only.
A program may use at most 256 MiB of HBM per device.

```python
import jax
import jax.numpy as jnp
from jax import lax

D = 768
HEADS = 12
HEAD_DIM = 64
FF = 3072
SEQ_DP = 2
DOC_MIN = 200
DOC_MAX = 2000
LENGTH = 1024
SEQS = 8
N_DP = 4


def draw_segment_ids(key, part):
    key = jax.random.fold_in(key, 7)
    length_key, pick_key = jax.random.split(key)
    doc_count = LENGTH // DOC_MIN + 1
    sizes_drawn = jax.random.randint(length_key, (SEQS, doc_count), DOC_MIN, DOC_MAX + 1)
    doc_ends = jnp.cumsum(sizes_drawn, axis=1)
    places = jnp.arange(LENGTH)
    doc_ids = jnp.sum((doc_ends[:, :, None] <= places[None, None, :]).astype(jnp.int32), axis=1)
    chosen = jax.random.randint(pick_key, (N_DP,), 0, SEQ_DP)
    seq_rows = jnp.arange(SEQS)
    whole_doc = seq_rows % SEQ_DP == chosen[seq_rows // SEQ_DP]
    shortest = seq_rows == (chosen[0] + 1) % SEQ_DP
    even_ids = (places // DOC_MIN).astype(jnp.int32)
    doc_ids = jnp.where(shortest[:, None], even_ids[None, :], doc_ids)
    return jnp.where(whole_doc[:, None], 0, doc_ids).astype(jnp.int32)


def block_levels(own_key, shape, pieces, smallest, top_value):
    loudness = 1.0
    for dim, parts in pieces:
        heights = jax.random.uniform(jax.random.fold_in(jax.random.fold_in(own_key, 6), dim), (parts,), jnp.float32, smallest / len(pieces), top_value / len(pieces))
        loudness = loudness * jnp.repeat(jnp.exp(heights), shape[dim] // parts).reshape((-1,) + (1,) * (len(shape) - 1 - dim))
    return loudness


def gaussian(own_key, dims, deviation, bound, cuts=(), dtype=jnp.bfloat16):
    loudness = block_levels(own_key, dims, cuts, -0.22, 0.18) if cuts else 1.0
    entries = jax.random.normal(own_key, dims, jnp.float32) * deviation * loudness
    return jnp.minimum(jnp.maximum(entries, -bound), bound).astype(dtype)


def setup_inputs(seed: int = 0) -> dict:
    splits = jax.random.split(jax.random.key(seed), 19)
    hidden_in = gaussian(splits[0], (SEQS, LENGTH, D), 1.0, 6.0, ((0, 4), (1, 8)))
    cotangent = gaussian(splits[1], (SEQS, LENGTH, D), 1.0, 6.0, ((0, 4), (1, 8)))
    segment_ids = draw_segment_ids(jax.random.fold_in(splits[18], 71), 0)
    query_weight = gaussian(splits[3], (D, D), D ** -0.5, 0.21875, ((0, 32),))
    key_weight = gaussian(splits[4], (D, D), D ** -0.5, 0.21875, ((0, 32),))
    value_weight = gaussian(splits[5], (D, D), D ** -0.5, 0.21875, ((0, 32),))
    out_weight = gaussian(splits[6], (D, D), (D // 32) ** -0.5, 1.25, ((0, 32),))
    up_weight = gaussian(splits[7], (D, FF), D ** -0.5, 0.21875, ((0, 32),))
    down_weight = gaussian(splits[8], (FF, D), FF ** -0.5, 0.109375, ((0, 32),))
    query_bias = gaussian(splits[9], (D,), 0.3, 1.796875, ((0, 32),))
    value_bias = gaussian(splits[10], (D,), 0.3, 1.796875, ((0, 32),))
    out_bias = gaussian(splits[11], (D,), 0.3, 1.796875, ((0, 32),))
    up_bias = gaussian(splits[12], (FF,), 0.3, 1.796875, ((0, 32),))
    down_bias = gaussian(splits[13], (D,), 0.3, 1.796875, ((0, 32),))
    first_gain = jnp.clip(1.0 + 0.1 * jax.random.normal(splits[14], (D,), jnp.float32), 0.5, 1.5).astype(jnp.bfloat16)
    first_shift = gaussian(splits[15], (D,), 0.3, 1.796875, ((0, 32),))
    second_gain = jnp.clip(1.0 + 0.1 * jax.random.normal(splits[16], (D,), jnp.float32), 0.5, 1.5).astype(jnp.bfloat16)
    second_shift = gaussian(splits[17], (D,), 0.3, 1.796875, ((0, 32),))
    return dict(hidden_in=hidden_in, cotangent=cotangent, segment_ids=segment_ids, query_weight=query_weight, key_weight=key_weight, value_weight=value_weight, out_weight=out_weight, up_weight=up_weight, down_weight=down_weight, query_bias=query_bias, value_bias=value_bias, out_bias=out_bias, up_bias=up_bias, down_bias=down_bias, first_gain=first_gain, first_shift=first_shift, second_gain=second_gain, second_shift=second_shift)


@jax.custom_vjp
def low(v):
    return lax.optimization_barrier(v.astype(jnp.bfloat16)).astype(jnp.float32)

@jax.custom_vjp
def low_back(v):
    return v

def low_keep(v):
    return (low(v), None)

def low_pass(kept, grad):
    return (grad,)

def back_keep(v):
    return (v, None)

def back_low(kept, grad):
    return (low(grad),)
low.defvjp(low_keep, low_pass)
low_back.defvjp(back_keep, back_low)

def layer_norm(value, gain, shift):
    center = value - lax.optimization_barrier(jnp.mean(value, -1, keepdims=True))
    spread = lax.optimization_barrier(jnp.mean(center * center, -1, keepdims=True))
    return center * lax.rsqrt(spread + 1e-05) * gain + shift

def matmul_hi(left, right):
    return jnp.dot(left, right, precision=lax.Precision.HIGHEST)

def attend(queries, keys, values, seg_row):
    seq_len = queries.shape[0]
    block_rows = min(512, seq_len)
    blocks = seq_len // block_rows
    places = jnp.arange(seq_len)

    def one_block(items):
        query_block, seg_block, place_block = items
        scores = jnp.einsum('qhd,khd->hqk', query_block, keys, precision=lax.Precision.HIGHEST)
        scores = low_back(scores)
        allowed = (seg_block[:, None] == seg_row[None, :]) & (places[None, :] <= place_block[:, None])
        scores = jnp.where(allowed[None], scores, -1000000000.0)
        scores = scores - lax.optimization_barrier(jnp.max(scores, -1, keepdims=True))
        expo = jnp.exp(scores)
        probs = low(expo / lax.optimization_barrier(jnp.sum(expo, -1, keepdims=True)))
        return jnp.einsum('hqk,khd->qhd', probs, values, precision=lax.Precision.HIGHEST)
    parted = lax.map(jax.checkpoint(one_block), (queries.reshape(blocks, block_rows, HEADS, HEAD_DIM), seg_row.reshape(blocks, block_rows), places.reshape(blocks, block_rows)))
    return parted.reshape(seq_len, HEADS * HEAD_DIM)

def forward(weights_all, block_in, seg_row):
    query_weight, key_weight, value_weight, out_weight, up_weight, down_weight, query_bias, value_bias, out_bias, up_bias, down_bias, first_gain, first_shift, second_gain, second_shift = weights_all
    seq_len = block_in.shape[0]
    normed = low(layer_norm(block_in, first_gain, first_shift))
    queries = low(low_back((matmul_hi(normed, query_weight) + query_bias) * 0.125))
    keys = low(low_back(matmul_hi(normed, key_weight)))
    values = low(low_back(matmul_hi(normed, value_weight) + value_bias))
    attended = attend(queries.reshape(seq_len, HEADS, HEAD_DIM), keys.reshape(seq_len, HEADS, HEAD_DIM), values.reshape(seq_len, HEADS, HEAD_DIM), seg_row)
    attended = low(low_back(attended))
    middle = block_in + low_back(matmul_hi(attended, out_weight) + out_bias)
    second_normed = low(layer_norm(middle, second_gain, second_shift))
    upper = low_back(matmul_hi(second_normed, up_weight) + up_bias)
    act = low(jax.nn.gelu(upper))
    return middle + low_back(matmul_hi(act, down_weight) + down_bias)

def reference(hidden_in, cotangent, segment_ids, query_weight, key_weight, value_weight, out_weight, up_weight, down_weight, query_bias, value_bias, out_bias, up_bias, down_bias, first_gain, first_shift, second_gain, second_shift):
    weights_all = tuple((item.astype(jnp.float32) for item in (query_weight, key_weight, value_weight, out_weight, up_weight, down_weight, query_bias, value_bias, out_bias, up_bias, down_bias, first_gain, first_shift, second_gain, second_shift)))

    def one_sequence(totals, items):
        block_in, block_grad, seg_row = items
        output_rows, back = jax.vjp(lambda held, rows_in: forward(held, rows_in, seg_row), weights_all, block_in.astype(jnp.float32))
        grad_weights, grad_rows = back(block_grad.astype(jnp.float32))
        totals = tuple((left + right for left, right in zip(totals, grad_weights)))
        return (totals, (output_rows.astype(jnp.bfloat16), grad_rows))
    zeros_all = tuple((jnp.zeros(item.shape, jnp.float32) for item in weights_all))
    totals, (outputs, grad_inputs) = lax.scan(one_sequence, zeros_all, (hidden_in, cotangent, segment_ids))
    return (outputs, grad_inputs) + tuple(totals)
```

```python
import jax
import jax.numpy as jnp
from jax import lax
from jax.sharding import PartitionSpec as P

HEADS = 12
HEAD_DIM = 64
MICRO = 2


def layer_norm(value, gain, shift):
    center = value - jnp.mean(value, -1, keepdims=True)
    spread = jnp.mean(center * center, -1, keepdims=True)
    return center * lax.rsqrt(spread + 1e-05) * gain + shift


def project(left, weight):
    return jnp.einsum("spd,de->spe", left, weight, preferred_element_type=jnp.float32)


def project_back(left, weight):
    return jnp.einsum("spe,de->spd", left, weight, preferred_element_type=jnp.float32)


def weight_term(left, right):
    return jnp.einsum("spd,spe->de", left, right, preferred_element_type=jnp.float32)


def row_total(value):
    return jnp.sum(value.astype(jnp.float32), axis=(0, 1))


def wide_local(
    hidden_in,
    cotangent,
    segment_ids,
    query_weight,
    key_weight,
    value_weight,
    out_weight,
    up_weight,
    down_weight,
    query_bias,
    value_bias,
    out_bias,
    up_bias,
    down_bias,
    first_gain,
    first_shift,
    second_gain,
    second_shift,
):
    params = (
        query_weight,
        key_weight,
        value_weight,
        out_weight,
        up_weight,
        down_weight,
        query_bias,
        value_bias,
        out_bias,
        up_bias,
        down_bias,
        first_gain,
        first_shift,
        second_gain,
        second_shift,
    )
    local_seqs, shard_rows, model_width = hidden_in.shape
    group_size = local_seqs // MICRO
    owners = lax.axis_size("dp") * lax.axis_size("seq")
    seg_all = lax.all_gather(segment_ids, "seq", axis=1, tiled=True)
    query_pos = lax.axis_index("seq") * shard_rows + jnp.arange(shard_rows)
    totals = tuple(
        (jnp.zeros((item.shape[0] * owners,) + item.shape[1:], jnp.float32) for item in params)
    )
    outs_rows = []
    outs_grads = []
    for micro_step in range(MICRO):
        lower = micro_step * group_size
        upper_end = lower + group_size
        gathered = (
            lax.all_gather(params[0], ("dp", "seq"), axis=0, tiled=True),
            lax.all_gather(params[1], ("dp", "seq"), axis=0, tiled=True),
            lax.all_gather(params[2], ("dp", "seq"), axis=0, tiled=True),
            lax.all_gather(params[3], ("dp", "seq"), axis=0, tiled=True),
            lax.all_gather(params[4], ("dp", "seq"), axis=0, tiled=True),
            lax.all_gather(params[5], ("dp", "seq"), axis=0, tiled=True),
            lax.all_gather(params[6], ("dp", "seq"), axis=0, tiled=True),
            lax.all_gather(params[7], ("dp", "seq"), axis=0, tiled=True),
            lax.all_gather(params[8], ("dp", "seq"), axis=0, tiled=True),
            lax.all_gather(params[9], ("dp", "seq"), axis=0, tiled=True),
            lax.all_gather(params[10], ("dp", "seq"), axis=0, tiled=True),
            lax.all_gather(params[11], ("dp", "seq"), axis=0, tiled=True),
            lax.all_gather(params[12], ("dp", "seq"), axis=0, tiled=True),
            lax.all_gather(params[13], ("dp", "seq"), axis=0, tiled=True),
            lax.all_gather(params[14], ("dp", "seq"), axis=0, tiled=True),
        )
        wq, wk, wv, wo, wu, wd = gathered[:6]
        bq, bv, bo, bu, bd, gain_one, shift_one, gain_two, shift_two = tuple(
            (item.astype(jnp.float32) for item in gathered[6:])
        )
        block_in = hidden_in[lower:upper_end].astype(jnp.float32)
        seg_here = segment_ids[lower:upper_end]
        seg_keys = seg_all[lower:upper_end]
        normed_low = layer_norm(block_in, gain_one, shift_one).astype(jnp.bfloat16)
        queries = (
            ((project(normed_low, wq) + bq) * 0.125)
            .astype(jnp.bfloat16)
            .reshape(group_size, shard_rows, HEADS, HEAD_DIM)
        )
        key_rows = project(normed_low, wk).astype(jnp.bfloat16)
        value_rows = (project(normed_low, wv) + bv).astype(jnp.bfloat16)

        def masked_scores(key_heads):
            count_keys = key_heads.shape[1]
            raw_scores = jnp.einsum(
                "sqhd,skhd->shqk", queries, key_heads, preferred_element_type=jnp.float32
            )
            key_pos = jnp.arange(count_keys)
            same_doc = seg_here[:, :, None] == seg_keys[:, None, :]
            causal = key_pos[None, :] <= query_pos[:, None]
            allowed = (same_doc & causal[None])[:, None]
            return jnp.where(allowed, raw_scores, -1000000000.0)

        pieces = (
            lax.all_gather(key_rows, "seq", axis=1, tiled=True),
            lax.all_gather(value_rows, "seq", axis=1, tiled=True),
        )
        run_max = jnp.full((group_size, HEADS, shard_rows), -1e30, jnp.float32)
        forward_count_keys = pieces[0].shape[1]
        forward_key_heads = pieces[0].reshape(group_size, forward_count_keys, HEADS, HEAD_DIM)
        value_heads = pieces[1].reshape(group_size, forward_count_keys, HEADS, HEAD_DIM)
        forward_raw_scores = masked_scores(forward_key_heads)
        new_max = jnp.maximum(run_max, jnp.max(forward_raw_scores, -1))
        expo = jnp.exp(forward_raw_scores - new_max[..., None])
        run_sum = jnp.sum(expo, -1)
        run_acc = jnp.einsum(
            "shqk,skhd->shqd",
            expo.astype(jnp.bfloat16),
            value_heads,
            preferred_element_type=jnp.float32,
        )
        run_max, run_sum, run_acc = (new_max, run_sum, run_acc)
        attended_full = (run_acc / run_sum[..., None]).transpose(0, 2, 1, 3)
        log_total = run_max + jnp.log(run_sum)
        attended_low = attended_full.reshape(group_size, shard_rows, model_width).astype(
            jnp.bfloat16
        )
        middle = block_in + project(attended_low, wo) + bo
        second_low = layer_norm(middle, gain_two, shift_two).astype(jnp.bfloat16)
        upper_pre = project(second_low, wu) + bu
        act_full, act_back = jax.vjp(jax.nn.gelu, upper_pre)
        act_low = act_full.astype(jnp.bfloat16)
        output_rows = middle + project(act_low, wd) + bd
        outs_rows.append(output_rows.astype(jnp.bfloat16))
        grad_out = cotangent[lower:upper_end].astype(jnp.float32)
        grad_low = grad_out.astype(jnp.bfloat16)
        d_act = project_back(grad_low, wd)
        d_upper = act_back(d_act)[0].astype(jnp.bfloat16)
        d_second = project_back(d_upper, wu)
        second_norm_back = jax.vjp(layer_norm, middle, gain_two, shift_two)[1]
        d_middle_part, d_gain_two, d_shift_two = second_norm_back(d_second)
        d_middle = grad_out + d_middle_part
        d_branch = d_middle.astype(jnp.bfloat16)
        d_attended = (
            project_back(d_branch, wo)
            .astype(jnp.bfloat16)
            .reshape(group_size, shard_rows, HEADS, HEAD_DIM)
        )
        row_dots = jnp.sum(d_attended.astype(jnp.float32) * attended_full, -1).transpose(0, 2, 1)
        backward_pieces = pieces
        backward_count_keys = backward_pieces[0].shape[1]
        backward_key_heads = backward_pieces[0].reshape(
            group_size, backward_count_keys, HEADS, HEAD_DIM
        )
        backward_value_heads = backward_pieces[1].reshape(
            group_size, backward_count_keys, HEADS, HEAD_DIM
        )
        probs = jnp.exp(masked_scores(backward_key_heads) - log_total[..., None])
        d_probs = jnp.einsum(
            "sqhd,skhd->shqk", d_attended, backward_value_heads, preferred_element_type=jnp.float32
        )
        d_scores = (probs * (d_probs - row_dots[..., None])).astype(jnp.bfloat16)
        value_term = jnp.einsum(
            "shqk,sqhd->skhd",
            probs.astype(jnp.bfloat16),
            d_attended,
            preferred_element_type=jnp.float32,
        )
        key_term = jnp.einsum(
            "shqk,sqhd->skhd", d_scores, queries, preferred_element_type=jnp.float32
        )
        d_query = jnp.einsum(
            "shqk,skhd->sqhd", d_scores, backward_key_heads, preferred_element_type=jnp.float32
        )
        d_keys_all = key_term.reshape(group_size, backward_count_keys, model_width)
        d_values_all = value_term.reshape(group_size, backward_count_keys, model_width)
        d_query, d_keys_all, d_values_all = (d_query, d_keys_all, d_values_all)
        d_keys, d_values = (
            lax.psum_scatter(
                d_keys_all.astype(jnp.bfloat16), "seq", scatter_dimension=1, tiled=True
            ).astype(jnp.float32),
            lax.psum_scatter(
                d_values_all.astype(jnp.bfloat16), "seq", scatter_dimension=1, tiled=True
            ).astype(jnp.float32),
        )
        d_query_low = d_query.reshape(group_size, shard_rows, model_width).astype(jnp.bfloat16)
        d_keys_low = d_keys.astype(jnp.bfloat16)
        d_values_low = d_values.astype(jnp.bfloat16)
        d_first = (
            0.125 * project_back(d_query_low, wq)
            + project_back(d_keys_low, wk)
            + project_back(d_values_low, wv)
        )
        first_norm_back = jax.vjp(layer_norm, block_in, gain_one, shift_one)[1]
        d_input_part, d_gain_one, d_shift_one = first_norm_back(d_first)
        outs_grads.append(d_middle + d_input_part)
        grad_terms = (
            0.125 * weight_term(normed_low, d_query_low),
            weight_term(normed_low, d_keys_low),
            weight_term(normed_low, d_values_low),
            weight_term(attended_low, d_branch),
            weight_term(second_low, d_upper),
            weight_term(act_low, grad_low),
            0.125 * row_total(d_query_low),
            row_total(d_values_low),
            row_total(d_branch),
            row_total(d_upper),
            row_total(grad_low),
            d_gain_one,
            d_shift_one,
            d_gain_two,
            d_shift_two,
        )
        totals = tuple((left + right for left, right in zip(totals, grad_terms)))
    grads = lax.psum_scatter(totals, ("dp", "seq"), scatter_dimension=0, tiled=True)
    return (jnp.concatenate(outs_rows, 0), jnp.concatenate(outs_grads, 0)) + tuple(grads)


CORE, NEAR_X, NEAR_Y = 1, 2, 4
GROUPS = 4


def swap(value, bit):
    return lax.ppermute(value, "seq", [(item, item ^ bit) for item in range(8)])


def pick(value, index, axis=0):
    return lax.dynamic_index_in_dim(value, index, axis, keepdims=False)


def in_order(own, other, bit, axis):
    return jnp.where(
        bit == 0, jnp.stack([own, other], axis), jnp.stack([other, own], axis)
    )


def spread(value):
    first, second = value[0], value[1]
    first = jnp.stack([first, swap(first, NEAR_X)])
    second = jnp.stack([second, swap(second, NEAR_Y)])
    first = jnp.concatenate([first, swap(first, NEAR_Y)])
    second = jnp.concatenate([second, swap(second, NEAR_X)])
    chip = jnp.stack([first, second])
    return jnp.stack([chip, swap(chip, CORE)])


def collect(value):
    chip = value[0] + swap(value[1], CORE)
    first, second = chip[0], chip[1]
    first = first[:2] + swap(first[2:], NEAR_Y)
    second = second[:2] + swap(second[2:], NEAR_X)
    first = first[0] + swap(first[1], NEAR_X)
    second = second[0] + swap(second[1], NEAR_Y)
    return jnp.stack([first, second])


def column_gather(value, place, count):
    parts = [value]
    for shift in range(1, count):
        parts.append(
            lax.ppermute(value, "dp", [(item, (item + shift) % count) for item in range(count)])
        )
    parts = jnp.stack(parts)
    ordered = [pick(parts, (place - item) % count) for item in range(count)]
    return jnp.concatenate(ordered)


def column_sum(value, place, count):
    total = pick(value, place).astype(jnp.float32)
    for shift in range(1, count):
        sent = pick(value, (place + shift) % count)
        total = total + lax.ppermute(
            sent, "dp", [(item, (item + shift) % count) for item in range(count)]
        ).astype(jnp.float32)
    return total


def norm_parts(value):
    center = value - jnp.mean(value, -1, keepdims=True)
    spread_rows = jnp.mean(center * center, -1, keepdims=True)
    scale = lax.rsqrt(spread_rows + 1e-05)
    return center * scale, scale


def norm_back(normal, scale, gain, grad):
    through = grad * gain
    kept = through - jnp.mean(through, -1, keepdims=True)
    kept = kept - normal * jnp.mean(through * normal, -1, keepdims=True)
    rows = tuple(range(grad.ndim - 1))
    return scale * kept, jnp.sum(grad * normal, rows), jnp.sum(grad, rows)


def dot(left, right):
    return jnp.dot(left, right, preferred_element_type=jnp.float32)


def dot_right(left, right):
    return lax.dot_general(
        left, right, (((1,), (1,)), ((), ())), preferred_element_type=jnp.float32
    )


def dot_left(left, right):
    return lax.dot_general(
        left, right, (((0,), (0,)), ((), ())), preferred_element_type=jnp.float32
    )


def attend_scores(queries, keys, allowed):
    scores = jnp.einsum("qhd,khd->hqk", queries, keys, preferred_element_type=jnp.float32)
    return jnp.where(allowed, scores, -1000000000.0)


def attend(queries, keys, values, segments):
    length = queries.shape[0]
    places = jnp.arange(length)
    allowed = (places[None, :] <= places[:, None]) & (segments[:, None] == segments[None, :])
    scores = attend_scores(queries, keys, allowed)
    top = jnp.max(scores, -1, keepdims=True)
    expo = jnp.exp(scores - top)
    total = jnp.sum(expo, -1, keepdims=True)
    out = jnp.einsum(
        "hqk,khd->hqd", expo.astype(jnp.bfloat16), values, preferred_element_type=jnp.float32
    )
    out = (out / total).transpose(1, 0, 2)
    return out, top + jnp.log(total), allowed


def attend_back(queries, keys, values, allowed, log_total, out, d_out):
    probs = jnp.exp(attend_scores(queries, keys, allowed) - log_total)
    row_dots = jnp.sum(d_out.astype(jnp.float32) * out, -1).T[..., None]
    d_probs = jnp.einsum("qhd,khd->hqk", d_out, values, preferred_element_type=jnp.float32)
    d_scores = (probs * (d_probs - row_dots)).astype(jnp.bfloat16)
    d_values = jnp.einsum(
        "hqk,qhd->khd", probs.astype(jnp.bfloat16), d_out, preferred_element_type=jnp.float32
    )
    d_keys = jnp.einsum("hqk,qhd->khd", d_scores, queries, preferred_element_type=jnp.float32)
    d_queries = jnp.einsum("hqk,khd->qhd", d_scores, keys, preferred_element_type=jnp.float32)
    return d_queries, d_keys, d_values


def plane_local(
    hidden_in,
    cotangent,
    segment_ids,
    query_weight,
    key_weight,
    value_weight,
    out_weight,
    up_weight,
    down_weight,
    query_bias,
    value_bias,
    out_bias,
    up_bias,
    down_bias,
    first_gain,
    first_shift,
    second_gain,
    second_shift,
):
    seqs, rows, width = hidden_in.shape
    plane = lax.axis_size("seq")
    columns = lax.axis_size("dp")
    owners = plane * columns
    share = query_weight.shape[0]
    ff_share = down_weight.shape[0]
    hidden = up_weight.shape[1]
    group_width = width // GROUPS
    group_heads = HEADS // GROUPS
    length = rows * plane
    place = lax.axis_index("seq")
    column = lax.axis_index("dp")
    bit_c, bit_x, bit_y = place % 2, (place // 2) % 2, place // 4
    group = place % GROUPS
    both = lambda item: jnp.concatenate([item, item])

    sent_qkv = jnp.stack([query_weight, key_weight, value_weight], 1)
    sent_qkv = sent_qkv.reshape(share, 3, GROUPS, group_width).transpose(2, 0, 1, 3)
    sent_qkv = both(sent_qkv.reshape(GROUPS, share, 3 * group_width))
    sent_up = up_weight.reshape(share, columns, plane, ff_share).transpose(2, 0, 1, 3)
    sent_up = sent_up.reshape(plane, share, columns * ff_share)
    per_row = -(-segment_ids.size // share)
    small = jnp.stack(
        [
            query_bias,
            value_bias,
            out_bias,
            down_bias,
            first_gain,
            first_shift,
            second_gain,
            second_shift,
        ],
        1,
    )
    numbers = segment_ids.astype(jnp.bfloat16).reshape(-1)
    numbers = jnp.pad(numbers, (0, per_row * share - numbers.size))
    small = jnp.concatenate(
        [small, up_bias.reshape(share, -1), numbers.reshape(share, per_row)], -1
    )
    bias_columns = ff_share // share
    small_width = small.shape[1]
    first_width = 3 * group_width + small_width
    small = jnp.broadcast_to(small, (plane,) + small.shape)
    got = lax.all_to_all(
        jnp.concatenate([sent_qkv, small, sent_up], -1), "seq", 0, 0, tiled=True
    ).reshape(plane * share, -1)
    first = column_gather(got[:, :first_width], column, columns)
    got_up = got[:, first_width:]
    half = plane * share // 2
    later = jnp.concatenate([jnp.concatenate([got_up[:half], got_up[half:]], -1), down_weight])
    first, later = lax.optimization_barrier((first, later))
    later = column_gather(later, column, columns).reshape(columns, 2 * half, width)
    w_up = jnp.concatenate(
        [later[:, :half, : width // 2], later[:, :half, width // 2 :]], 1
    ).reshape(width, columns * ff_share)
    w_down = later[:, half:].reshape(columns * ff_share, width)
    w_out = lax.all_gather(out_weight, ("dp", "seq"), axis=0, tiled=True)

    w_qkv = first[:, : 3 * group_width]
    small = first[:, 3 * group_width :]
    bq, bv, bo, bd, gain_one, shift_one, gain_two, shift_two = [
        small[:, i].astype(jnp.float32) for i in range(8)
    ]
    bu = small[:, 8 : 8 + bias_columns].reshape(columns, plane, ff_share)
    bu = pick(bu, place, 1).reshape(-1).astype(jnp.float32)
    segments = pick(small[:, 8 + bias_columns :].reshape(columns, plane, -1), column)
    segments = segments[:, : seqs * rows].reshape(plane, seqs, rows)
    segments = pick(segments, bit_y, 1).reshape(length)

    mine = pick(hidden_in, bit_y)
    mine = in_order(mine, swap(pick(hidden_in, 1 - bit_y), NEAR_Y), bit_y, 0)
    mine = in_order(mine, swap(mine, NEAR_X), bit_x, 1)
    mine = in_order(mine, swap(mine, CORE), bit_c, 2).reshape(length, width)
    grads_all = spread(cotangent).reshape(-1, width)

    normal_all, _ = norm_parts(mine.astype(jnp.float32))
    normed = (normal_all * gain_one + shift_one).astype(jnp.bfloat16)
    qkv = dot(normed, w_qkv)
    own_columns = lambda item: lax.dynamic_slice_in_dim(item, group * group_width, group_width)
    heads = lambda item: item.astype(jnp.bfloat16).reshape(length, group_heads, HEAD_DIM)
    queries = heads((qkv[:, :group_width] + own_columns(bq)) * 0.125)
    keys = heads(qkv[:, group_width : 2 * group_width])
    values = heads(qkv[:, 2 * group_width :] + own_columns(bv))
    out, log_total, allowed = attend(queries, keys, values, segments)

    attended = out.astype(jnp.bfloat16).reshape(plane, rows, group_width)
    attended, grads_all = lax.optimization_barrier((attended, grads_all))
    attended = lax.all_to_all(attended, "seq", 0, 0, tiled=True)
    attended = attended.reshape(seqs, GROUPS, rows, group_width).transpose(0, 2, 1, 3)
    attended = attended.reshape(seqs * rows, width)
    block_in = hidden_in.astype(jnp.float32).reshape(seqs * rows, width)
    middle = block_in + dot(attended, w_out) + bo
    normal_two, scale_two = norm_parts(middle)
    second = (normal_two * gain_two + shift_two).astype(jnp.bfloat16)
    second_all = spread(second.reshape(seqs, rows, width)).reshape(-1, width)

    upper = dot(second_all, w_up) + bu
    act, act_back = jax.vjp(jax.nn.gelu, upper)
    act = act.astype(jnp.bfloat16)
    d_upper = act_back(dot_right(grads_all, w_down))[0].astype(jnp.bfloat16)
    halves = lambda item: item.astype(jnp.bfloat16).reshape(2, 2, 4, rows, width)
    d_second = collect(halves(dot_right(d_upper, w_up))).reshape(seqs * rows, width)
    down = halves(dot(act, w_down))

    grad_up = dot_left(second_all, d_upper).astype(jnp.bfloat16)
    grad_up = grad_up.reshape(columns, 2, half, columns * ff_share)
    grad_down = dot_left(act, grads_all).astype(jnp.bfloat16).reshape(columns, ff_share, width)
    late = jnp.concatenate(
        [jnp.concatenate([grad_up[:, 0], grad_up[:, 1]], -1), grad_down], 1
    )
    late = column_sum(late, column, columns)
    grad_down = late[half:]
    grad_up = jnp.concatenate([late[:half, : width // 2], late[:half, width // 2 :]])

    own_grad = cotangent.astype(jnp.float32).reshape(seqs * rows, width)
    d_middle, d_gain_two, d_shift_two = norm_back(
        normal_two, scale_two, gain_two, d_second.astype(jnp.float32)
    )
    d_middle = own_grad + d_middle
    d_branch = d_middle.astype(jnp.bfloat16)
    grad_out = lax.psum_scatter(
        dot_left(attended, d_branch).astype(jnp.bfloat16),
        ("dp", "seq"),
        scatter_dimension=0,
        tiled=True,
    )
    d_attended = dot_right(d_branch, w_out).astype(jnp.bfloat16)
    d_attended = d_attended.reshape(seqs, rows, GROUPS, group_width).transpose(0, 2, 1, 3)
    d_attended = d_attended.reshape(plane, rows, group_width)
    d_attended = lax.all_to_all(d_attended, "seq", 0, 0, tiled=True)
    d_attended, down = lax.optimization_barrier((d_attended, down))
    down = collect(down).reshape(seqs * rows, width)
    hidden_out = (middle + down.astype(jnp.float32) + bd).astype(jnp.bfloat16)
    d_attended = d_attended.reshape(length, group_heads, HEAD_DIM)
    d_queries, d_keys, d_values = attend_back(
        queries, keys, values, allowed, log_total, out, d_attended
    )
    flat = lambda item: item.astype(jnp.bfloat16).reshape(length, group_width)
    d_queries, d_keys, d_values = flat(d_queries), flat(d_keys), flat(d_values)
    d_qkv = jnp.concatenate([d_queries * jnp.bfloat16(0.125), d_keys, d_values], -1)

    grad_qkv = dot_left(normed, d_qkv).astype(jnp.bfloat16)
    d_first = dot_right(d_qkv, w_qkv)

    def placed(item):
        zeros = jnp.zeros((width,), jnp.float32)
        return lax.dynamic_update_slice_in_dim(zeros, item, group * group_width, 0)

    total = lambda item: jnp.sum(item.astype(jnp.float32), 0)
    d_bu = lax.dynamic_update_index_in_dim(
        jnp.zeros((columns, plane, ff_share), jnp.float32),
        total(d_upper).reshape(columns, ff_share),
        place,
        1,
    ).reshape(width, bias_columns)
    terms = [
        placed(0.125 * total(d_queries)),
        placed(total(d_values)),
        total(d_branch),
        total(own_grad),
        total(d_first * normal_all),
        total(d_first),
        d_gain_two,
        d_shift_two,
    ]
    terms = jnp.concatenate([jnp.stack(terms, 1), d_bu], -1)
    coarse = lax.reduce_precision(terms, 8, 7)
    terms = jnp.concatenate([coarse, terms - coarse], -1).astype(jnp.bfloat16)
    last = jnp.concatenate([grad_qkv, terms], -1)
    last = column_sum(last.reshape(columns, plane * share, -1), column, columns)
    terms = last[:, 3 * group_width :]
    coarse = lax.reduce_precision(terms, 8, 7)
    last = jnp.concatenate([last[:, : 3 * group_width], coarse, terms - coarse, grad_up], -1)
    last = lax.all_to_all(
        last.astype(jnp.bfloat16).reshape(plane, share, -1), "seq", 0, 0, tiled=True
    ).astype(jnp.float32)
    grad_qkv = last[..., : 3 * group_width].reshape(2, GROUPS, share, 3, group_width)
    grad_qkv = jnp.sum(grad_qkv, 0).transpose(2, 1, 0, 3).reshape(3, share, width)
    grad_up = last[..., -columns * ff_share :].reshape(plane, share, columns, ff_share)
    grad_up = grad_up.transpose(1, 2, 0, 3).reshape(share, hidden)
    terms = jnp.sum(last[..., 3 * group_width : -columns * ff_share], 0)
    terms = jnp.sum(terms.reshape(share, 4, -1), 1)
    g_bq, g_bv, g_bo, g_bd, g_g1, g_s1, g_g2, g_s2 = [terms[:, i] for i in range(8)]
    g_bu = terms[:, 8:].reshape(-1)

    d_first = d_first.astype(jnp.bfloat16).reshape(2, 2, 2, rows, width)
    d_first = pick(d_first, bit_c, 2) + swap(pick(d_first, 1 - bit_c, 2), CORE)
    d_first = pick(d_first, bit_x, 1) + swap(pick(d_first, 1 - bit_x, 1), NEAR_X)
    d_first = in_order(pick(d_first, bit_y), swap(pick(d_first, 1 - bit_y), NEAR_Y), bit_y, 0)
    d_first = d_first.reshape(seqs * rows, width).astype(jnp.float32)
    normal_one, scale_one = norm_parts(block_in)
    d_input, _, _ = norm_back(normal_one, scale_one, gain_one, d_first)
    grad_input = (d_middle + d_input).reshape(seqs, rows, width)

    return (
        hidden_out.reshape(seqs, rows, width),
        grad_input,
        grad_qkv[0],
        grad_qkv[1],
        grad_qkv[2],
        grad_out.astype(jnp.float32),
        grad_up,
        grad_down,
        g_bq,
        g_bv,
        g_bo,
        g_bu,
        g_bd,
        g_g1,
        g_s1,
        g_g2,
        g_s2,
    )


def solution(mesh):
    plane = mesh.shape["seq"] == 8 and HEADS % 4 == 0
    body = plane_local if plane else wide_local
    placed = (
        P("dp", "seq", None),
        P("dp", "seq", None),
        P("dp", "seq"),
        P(("dp", "seq"), None),
        P(("dp", "seq"), None),
        P(("dp", "seq"), None),
        P(("dp", "seq"), None),
        P(("dp", "seq"), None),
        P(("dp", "seq"), None),
        P(("dp", "seq")),
        P(("dp", "seq")),
        P(("dp", "seq")),
        P(("dp", "seq")),
        P(("dp", "seq")),
        P(("dp", "seq")),
        P(("dp", "seq")),
        P(("dp", "seq")),
        P(("dp", "seq")),
    )
    return jax.shard_map(
        body,
        mesh=mesh,
        in_specs=placed,
        out_specs=(
            P("dp", "seq", None),
            P("dp", "seq", None),
            P(("dp", "seq"), None),
            P(("dp", "seq"), None),
            P(("dp", "seq"), None),
            P(("dp", "seq"), None),
            P(("dp", "seq"), None),
            P(("dp", "seq"), None),
            P(("dp", "seq")),
            P(("dp", "seq")),
            P(("dp", "seq")),
            P(("dp", "seq")),
            P(("dp", "seq")),
            P(("dp", "seq")),
            P(("dp", "seq")),
            P(("dp", "seq")),
            P(("dp", "seq")),
        ),
        check_vma=False,
    )
```

```python
import jax
import jax.numpy as jnp
from jax import lax
from jax.experimental import pallas as pl
from jax.experimental.pallas import tpu as pltpu
from jax.sharding import PartitionSpec as P

HEADS = 12
HEAD_DIM = 64
MICRO = 2


def layer_norm(value, gain, shift):
    center = value - jnp.mean(value, -1, keepdims=True)
    spread = jnp.mean(center * center, -1, keepdims=True)
    return center * lax.rsqrt(spread + 1e-05) * gain + shift


def project(left, weight):
    return jnp.einsum("spd,de->spe", left, weight, preferred_element_type=jnp.float32)


def project_back(left, weight):
    return jnp.einsum("spe,de->spd", left, weight, preferred_element_type=jnp.float32)


def weight_term(left, right):
    return jnp.einsum("spd,spe->de", left, right, preferred_element_type=jnp.float32)


def row_total(value):
    return jnp.sum(value.astype(jnp.float32), axis=(0, 1))


def wide_local(
    hidden_in,
    cotangent,
    segment_ids,
    query_weight,
    key_weight,
    value_weight,
    out_weight,
    up_weight,
    down_weight,
    query_bias,
    value_bias,
    out_bias,
    up_bias,
    down_bias,
    first_gain,
    first_shift,
    second_gain,
    second_shift,
):
    params = (
        query_weight,
        key_weight,
        value_weight,
        out_weight,
        up_weight,
        down_weight,
        query_bias,
        value_bias,
        out_bias,
        up_bias,
        down_bias,
        first_gain,
        first_shift,
        second_gain,
        second_shift,
    )
    local_seqs, shard_rows, model_width = hidden_in.shape
    group_size = local_seqs // MICRO
    owners = lax.axis_size("dp") * lax.axis_size("seq")
    seg_all = lax.all_gather(segment_ids, "seq", axis=1, tiled=True)
    query_pos = lax.axis_index("seq") * shard_rows + jnp.arange(shard_rows)
    totals = tuple(
        (jnp.zeros((item.shape[0] * owners,) + item.shape[1:], jnp.float32) for item in params)
    )
    outs_rows = []
    outs_grads = []
    for micro_step in range(MICRO):
        lower = micro_step * group_size
        upper_end = lower + group_size
        gathered = (
            lax.all_gather(params[0], ("dp", "seq"), axis=0, tiled=True),
            lax.all_gather(params[1], ("dp", "seq"), axis=0, tiled=True),
            lax.all_gather(params[2], ("dp", "seq"), axis=0, tiled=True),
            lax.all_gather(params[3], ("dp", "seq"), axis=0, tiled=True),
            lax.all_gather(params[4], ("dp", "seq"), axis=0, tiled=True),
            lax.all_gather(params[5], ("dp", "seq"), axis=0, tiled=True),
            lax.all_gather(params[6], ("dp", "seq"), axis=0, tiled=True),
            lax.all_gather(params[7], ("dp", "seq"), axis=0, tiled=True),
            lax.all_gather(params[8], ("dp", "seq"), axis=0, tiled=True),
            lax.all_gather(params[9], ("dp", "seq"), axis=0, tiled=True),
            lax.all_gather(params[10], ("dp", "seq"), axis=0, tiled=True),
            lax.all_gather(params[11], ("dp", "seq"), axis=0, tiled=True),
            lax.all_gather(params[12], ("dp", "seq"), axis=0, tiled=True),
            lax.all_gather(params[13], ("dp", "seq"), axis=0, tiled=True),
            lax.all_gather(params[14], ("dp", "seq"), axis=0, tiled=True),
        )
        wq, wk, wv, wo, wu, wd = gathered[:6]
        bq, bv, bo, bu, bd, gain_one, shift_one, gain_two, shift_two = tuple(
            (item.astype(jnp.float32) for item in gathered[6:])
        )
        block_in = hidden_in[lower:upper_end].astype(jnp.float32)
        seg_here = segment_ids[lower:upper_end]
        seg_keys = seg_all[lower:upper_end]
        normed_low = layer_norm(block_in, gain_one, shift_one).astype(jnp.bfloat16)
        queries = (
            ((project(normed_low, wq) + bq) * 0.125)
            .astype(jnp.bfloat16)
            .reshape(group_size, shard_rows, HEADS, HEAD_DIM)
        )
        key_rows = project(normed_low, wk).astype(jnp.bfloat16)
        value_rows = (project(normed_low, wv) + bv).astype(jnp.bfloat16)

        def masked_scores(key_heads):
            count_keys = key_heads.shape[1]
            raw_scores = jnp.einsum(
                "sqhd,skhd->shqk", queries, key_heads, preferred_element_type=jnp.float32
            )
            key_pos = jnp.arange(count_keys)
            same_doc = seg_here[:, :, None] == seg_keys[:, None, :]
            causal = key_pos[None, :] <= query_pos[:, None]
            allowed = (same_doc & causal[None])[:, None]
            return jnp.where(allowed, raw_scores, -1000000000.0)

        pieces = (
            lax.all_gather(key_rows, "seq", axis=1, tiled=True),
            lax.all_gather(value_rows, "seq", axis=1, tiled=True),
        )
        run_max = jnp.full((group_size, HEADS, shard_rows), -1e30, jnp.float32)
        forward_count_keys = pieces[0].shape[1]
        forward_key_heads = pieces[0].reshape(group_size, forward_count_keys, HEADS, HEAD_DIM)
        value_heads = pieces[1].reshape(group_size, forward_count_keys, HEADS, HEAD_DIM)
        forward_raw_scores = masked_scores(forward_key_heads)
        new_max = jnp.maximum(run_max, jnp.max(forward_raw_scores, -1))
        expo = jnp.exp(forward_raw_scores - new_max[..., None])
        run_sum = jnp.sum(expo, -1)
        run_acc = jnp.einsum(
            "shqk,skhd->shqd",
            expo.astype(jnp.bfloat16),
            value_heads,
            preferred_element_type=jnp.float32,
        )
        run_max, run_sum, run_acc = (new_max, run_sum, run_acc)
        attended_full = (run_acc / run_sum[..., None]).transpose(0, 2, 1, 3)
        log_total = run_max + jnp.log(run_sum)
        attended_low = attended_full.reshape(group_size, shard_rows, model_width).astype(
            jnp.bfloat16
        )
        middle = block_in + project(attended_low, wo) + bo
        second_low = layer_norm(middle, gain_two, shift_two).astype(jnp.bfloat16)
        upper_pre = project(second_low, wu) + bu
        act_full, act_back = jax.vjp(jax.nn.gelu, upper_pre)
        act_low = act_full.astype(jnp.bfloat16)
        output_rows = middle + project(act_low, wd) + bd
        outs_rows.append(output_rows.astype(jnp.bfloat16))
        grad_out = cotangent[lower:upper_end].astype(jnp.float32)
        grad_low = grad_out.astype(jnp.bfloat16)
        d_act = project_back(grad_low, wd)
        d_upper = act_back(d_act)[0].astype(jnp.bfloat16)
        d_second = project_back(d_upper, wu)
        second_norm_back = jax.vjp(layer_norm, middle, gain_two, shift_two)[1]
        d_middle_part, d_gain_two, d_shift_two = second_norm_back(d_second)
        d_middle = grad_out + d_middle_part
        d_branch = d_middle.astype(jnp.bfloat16)
        d_attended = (
            project_back(d_branch, wo)
            .astype(jnp.bfloat16)
            .reshape(group_size, shard_rows, HEADS, HEAD_DIM)
        )
        row_dots = jnp.sum(d_attended.astype(jnp.float32) * attended_full, -1).transpose(0, 2, 1)
        backward_pieces = pieces
        backward_count_keys = backward_pieces[0].shape[1]
        backward_key_heads = backward_pieces[0].reshape(
            group_size, backward_count_keys, HEADS, HEAD_DIM
        )
        backward_value_heads = backward_pieces[1].reshape(
            group_size, backward_count_keys, HEADS, HEAD_DIM
        )
        probs = jnp.exp(masked_scores(backward_key_heads) - log_total[..., None])
        d_probs = jnp.einsum(
            "sqhd,skhd->shqk", d_attended, backward_value_heads, preferred_element_type=jnp.float32
        )
        d_scores = (probs * (d_probs - row_dots[..., None])).astype(jnp.bfloat16)
        value_term = jnp.einsum(
            "shqk,sqhd->skhd",
            probs.astype(jnp.bfloat16),
            d_attended,
            preferred_element_type=jnp.float32,
        )
        key_term = jnp.einsum(
            "shqk,sqhd->skhd", d_scores, queries, preferred_element_type=jnp.float32
        )
        d_query = jnp.einsum(
            "shqk,skhd->sqhd", d_scores, backward_key_heads, preferred_element_type=jnp.float32
        )
        d_keys_all = key_term.reshape(group_size, backward_count_keys, model_width)
        d_values_all = value_term.reshape(group_size, backward_count_keys, model_width)
        d_query, d_keys_all, d_values_all = (d_query, d_keys_all, d_values_all)
        d_keys, d_values = (
            lax.psum_scatter(
                d_keys_all.astype(jnp.bfloat16), "seq", scatter_dimension=1, tiled=True
            ).astype(jnp.float32),
            lax.psum_scatter(
                d_values_all.astype(jnp.bfloat16), "seq", scatter_dimension=1, tiled=True
            ).astype(jnp.float32),
        )
        d_query_low = d_query.reshape(group_size, shard_rows, model_width).astype(jnp.bfloat16)
        d_keys_low = d_keys.astype(jnp.bfloat16)
        d_values_low = d_values.astype(jnp.bfloat16)
        d_first = (
            0.125 * project_back(d_query_low, wq)
            + project_back(d_keys_low, wk)
            + project_back(d_values_low, wv)
        )
        first_norm_back = jax.vjp(layer_norm, block_in, gain_one, shift_one)[1]
        d_input_part, d_gain_one, d_shift_one = first_norm_back(d_first)
        outs_grads.append(d_middle + d_input_part)
        grad_terms = (
            0.125 * weight_term(normed_low, d_query_low),
            weight_term(normed_low, d_keys_low),
            weight_term(normed_low, d_values_low),
            weight_term(attended_low, d_branch),
            weight_term(second_low, d_upper),
            weight_term(act_low, grad_low),
            0.125 * row_total(d_query_low),
            row_total(d_values_low),
            row_total(d_branch),
            row_total(d_upper),
            row_total(grad_low),
            d_gain_one,
            d_shift_one,
            d_gain_two,
            d_shift_two,
        )
        totals = tuple((left + right for left, right in zip(totals, grad_terms)))
    grads = lax.psum_scatter(totals, ("dp", "seq"), scatter_dimension=0, tiled=True)
    return (jnp.concatenate(outs_rows, 0), jnp.concatenate(outs_grads, 0)) + tuple(grads)


CORE, NEAR_X, NEAR_Y, ACROSS = 1, 2, 4, 6
GROUPS = 4


def tie(*values):
    return lax.optimization_barrier(values)


def swap(value, mask):
    return lax.ppermute(value, "seq", [(item, item ^ mask) for item in range(8)])


def pick(value, index, axis=0):
    return lax.dynamic_index_in_dim(value, index, axis, keepdims=False)


def in_order(own, other, bit, axis):
    return jnp.where(
        bit == 0, jnp.stack([own, other], axis), jnp.stack([other, own], axis)
    )


def plus(left, right):
    return (left.astype(jnp.float32) + right.astype(jnp.float32)).astype(jnp.bfloat16)


def total_of(parts):
    return sum(part.astype(jnp.float32) for part in parts)


def chips(value):
    return [value] + [swap(value, mask) for mask in (NEAR_X, NEAR_Y, ACROSS)]


def chips_send(order):
    got = [order(0)]
    for item, mask in ((1, NEAR_X), (2, NEAR_Y), (3, ACROSS)):
        got.append(swap(order(item), mask))
    return got


def chips_order(parts, chip):
    parts = jnp.stack(parts)
    return jnp.stack([pick(parts, chip ^ item) for item in range(GROUPS)])


def column_parts(value, count):
    parts = [value]
    for shift in range(1, count):
        perm = [(item, (item + shift) % count) for item in range(count)]
        parts.append(lax.ppermute(value, "dp", perm))
    return parts


def column_order(parts, place):
    count = len(parts)
    parts = jnp.stack(parts)
    return jnp.stack([pick(parts, (place - item) % count) for item in range(count)])


def column_send(value, place, count):
    parts = [pick(value, place)]
    for shift in range(1, count):
        sent = pick(value, (place + shift) % count)
        perm = [(item, (item + shift) % count) for item in range(count)]
        parts.append(lax.ppermute(sent, "dp", perm))
    return parts


def norm_parts(value):
    center = value - jnp.mean(value, -1, keepdims=True)
    spread_rows = jnp.mean(center * center, -1, keepdims=True)
    scale = lax.rsqrt(spread_rows + 1e-05)
    return center * scale, scale


def norm_back(normal, scale, gain, grad):
    through = grad * gain
    kept = through - jnp.mean(through, -1, keepdims=True)
    kept = kept - normal * jnp.mean(through * normal, -1, keepdims=True)
    return scale * kept


def dot(left, right):
    return jnp.dot(left, right, preferred_element_type=jnp.float32)


def dot_right(left, right):
    return lax.dot_general(
        left, right, (((1,), (1,)), ((), ())), preferred_element_type=jnp.float32
    )


def dot_left(left, right):
    return lax.dot_general(
        left, right, (((0,), (0,)), ((), ())), preferred_element_type=jnp.float32
    )


BLOCK = 256
VMEM_BYTES = 60 * 1024 * 1024


def head_mask(head, count):
    lane = lax.broadcasted_iota(jnp.int32, (1, count), 1)
    inside = (lane >= head * HEAD_DIM) & (lane < (head + 1) * HEAD_DIM)
    return inside.astype(jnp.float32).astype(jnp.bfloat16)


def head_rows(head):
    return pl.ds(pl.multiple_of(head * HEAD_DIM, HEAD_DIM), HEAD_DIM)


def flipped(value):
    return value.astype(jnp.float32).T.astype(jnp.bfloat16)


def attend_kernel(
    normed_ref, w_ref, bias_ref, row_ref, column_ref,
    q_ref, k_ref, v_ref, full_ref, out_ref, p_ref, v_flip, held,
):
    head = pl.program_id(0)
    length, count = q_ref.shape

    @pl.when(head == 0)
    def first():
        for start in range(0, length, BLOCK):
            rows = pl.ds(start, BLOCK)
            product = dot(normed_ref[rows], w_ref[...]) + bias_ref[...]
            q_ref[rows] = (product[:, :count] * 0.125).astype(jnp.bfloat16)
            k_ref[rows] = product[:, count : 2 * count].astype(jnp.bfloat16)
            v_ref[rows] = product[:, 2 * count :].astype(jnp.bfloat16)
        v_flip[...] = flipped(v_ref[...])

    mask = head_mask(head, count)
    for start in range(0, length, BLOCK):
        stop = start + BLOCK
        scores = dot_right(k_ref[:stop], q_ref[start:stop] * mask)
        shape = (stop, BLOCK)
        causal = lax.broadcasted_iota(jnp.int32, shape, 0) <= start + lax.broadcasted_iota(
            jnp.int32, shape, 1
        )
        same = column_ref[:stop] == row_ref[:, start:stop]
        scores = jnp.where(causal & same, scores, -1000000000.0)
        expo = jnp.exp(scores - jnp.max(scores, 0, keepdims=True))
        probs = (expo * (1.0 / jnp.sum(expo, 0, keepdims=True))).astype(jnp.bfloat16)
        p_ref[0, :stop, start:stop] = probs
        held[head_rows(head), start:stop] = dot(v_flip[head_rows(head), :stop], probs)

    @pl.when(head == pl.num_programs(0) - 1)
    def last():
        full = held[...].T
        full_ref[...] = full
        out_ref[...] = full.astype(jnp.bfloat16)


def attend_back_kernel(
    chip_ref, q_ref, k_ref, v_ref, d_ref, full_ref, normed_ref, w_ref, normal_ref, p_ref,
    grad_ref, first_ref, sums_ref, bias_ref, k_flip, dots, dq, dk, dv, d_all,
):
    head = pl.program_id(0)
    length, count = q_ref.shape

    @pl.when(head == 0)
    def first():
        k_flip[...] = flipped(k_ref[...])
        dots[...] = (d_ref[...].astype(jnp.float32) * full_ref[...]).T
        dk[...] = jnp.zeros_like(dk)
        dv[...] = jnp.zeros_like(dv)

    mask = head_mask(head, count)
    for start in range(0, length, BLOCK):
        stop = start + BLOCK
        d_out = d_ref[start:stop] * mask
        probs = p_ref[0, :stop, start:stop]
        row_dots = jnp.sum(dots[head_rows(head), start:stop], 0, keepdims=True)
        d_probs = dot_right(v_ref[:stop], d_out)
        d_scores = (probs.astype(jnp.float32) * (d_probs - row_dots)).astype(jnp.bfloat16)
        dv[:stop] += dot(probs, d_out)
        dk[:stop] += dot(d_scores, q_ref[start:stop] * mask)
        dq[head_rows(head), start:stop] = dot(k_flip[head_rows(head), :stop], d_scores)

    @pl.when(head == pl.num_programs(0) - 1)
    def last():
        for start in range(0, length, BLOCK):
            rows = pl.ds(start, BLOCK)
            d_queries = dq[:, start : start + BLOCK].T.astype(jnp.bfloat16).astype(jnp.float32)
            d_all[rows] = jnp.concatenate([d_queries * 0.125, dk[rows], dv[rows]], 1).astype(
                jnp.bfloat16
            )
        bias_ref[...] = jnp.sum(d_all[...].astype(jnp.float32), 0, keepdims=True)
        grad_ref[...] = dot_left(normed_ref[...], d_all[...]).astype(jnp.bfloat16)
        sums_ref[...] = jnp.zeros_like(sums_ref)
        for item in range(GROUPS):
            size = length // GROUPS
            rows = pl.ds(pl.multiple_of((chip_ref[0] ^ item) * size, size), size)
            d_first = dot_right(d_all[rows], w_ref[...])
            sums_ref[0:1] += jnp.sum(d_first * normal_ref[rows], 0, keepdims=True)
            sums_ref[1:2] += jnp.sum(d_first, 0, keepdims=True)
            first_ref[item] = d_first.astype(jnp.bfloat16)


def whole(*shape):
    return pl.BlockSpec(shape, lambda head: (0,) * len(shape))


def kernel_params():
    return pltpu.CompilerParams(
        dimension_semantics=("arbitrary",), vmem_limit_bytes=VMEM_BYTES
    )


def attend(normed, weights, bias, segments):
    length, width = normed.shape
    count = weights.shape[1] // 3
    heads = count // HEAD_DIM
    shape = (length, count)
    low = jax.ShapeDtypeStruct(shape, jnp.bfloat16)
    probs = pl.BlockSpec((1, length, length), lambda head: (head, 0, 0))
    queries, keys, values, full, out, probs = pl.pallas_call(
        attend_kernel,
        grid=(heads,),
        in_specs=[
            whole(length, width),
            whole(width, 3 * count),
            whole(1, 3 * count),
            whole(1, length),
            whole(length, 1),
        ],
        out_specs=[whole(*shape)] * 5 + [probs],
        out_shape=[
            low,
            low,
            low,
            jax.ShapeDtypeStruct(shape, jnp.float32),
            low,
            jax.ShapeDtypeStruct((heads, length, length), jnp.bfloat16),
        ],
        scratch_shapes=[
            pltpu.VMEM((count, length), jnp.bfloat16),
            pltpu.VMEM((count, length), jnp.float32),
        ],
        compiler_params=kernel_params(),
        cost_estimate=pl.CostEstimate(
            flops=4 * length * length * count + 6 * length * width * count,
            bytes_accessed=2 * heads * length * length,
            transcendentals=heads * length * length,
        ),
    )(normed, weights, bias[None], segments[None], segments[:, None])
    return out, (queries, keys, values), (full, probs)


def attend_back(chip, projected, kept, d_out, normed, weights, normal):
    length, width = normed.shape
    count = d_out.shape[1]
    heads = count // HEAD_DIM
    shape = (length, count)
    full, probs = kept
    size = length // GROUPS
    return pl.pallas_call(
        attend_back_kernel,
        grid=(heads,),
        in_specs=[pl.BlockSpec(memory_space=pltpu.SMEM)]
        + [whole(*shape)] * 5
        + [
            whole(length, width),
            whole(width, 3 * count),
            whole(length, width),
            pl.BlockSpec((1, length, length), lambda head: (head, 0, 0)),
        ],
        out_specs=[
            whole(width, 3 * count),
            whole(GROUPS, size, width),
            whole(8, width),
            whole(1, 3 * count),
        ],
        out_shape=[
            jax.ShapeDtypeStruct((width, 3 * count), jnp.bfloat16),
            jax.ShapeDtypeStruct((GROUPS, size, width), jnp.bfloat16),
            jax.ShapeDtypeStruct((8, width), jnp.float32),
            jax.ShapeDtypeStruct((1, 3 * count), jnp.float32),
        ],
        scratch_shapes=[
            pltpu.VMEM((count, length), jnp.bfloat16),
            pltpu.VMEM((count, length), jnp.float32),
            pltpu.VMEM((count, length), jnp.float32),
            pltpu.VMEM(shape, jnp.float32),
            pltpu.VMEM(shape, jnp.float32),
            pltpu.VMEM((length, 3 * count), jnp.bfloat16),
        ],
        compiler_params=kernel_params(),
        cost_estimate=pl.CostEstimate(
            flops=10 * length * length * count + 12 * length * width * count,
            bytes_accessed=2 * heads * length * length,
            transcendentals=0,
        ),
    )(chip[None], *projected, d_out, full, normed, weights, normal, probs)


def one(*shape):
    return jax.ShapeDtypeStruct(shape, jnp.float32)


def low(*shape):
    return jax.ShapeDtypeStruct(shape, jnp.bfloat16)


def run(body, given, outs, flops, scratch=(), scalars=()):
    specs = [pl.BlockSpec(memory_space=pltpu.SMEM)] * len(scalars)
    return pl.pallas_call(
        body,
        grid=(1,),
        in_specs=specs + [whole(*item.shape) for item in given],
        out_specs=[whole(*item.shape) for item in outs],
        out_shape=list(outs),
        scratch_shapes=list(scratch),
        compiler_params=pltpu.CompilerParams(vmem_limit_bytes=VMEM_BYTES),
        cost_estimate=pl.CostEstimate(flops=flops, bytes_accessed=0, transcendentals=0),
    )(*[item[None] for item in scalars], *given)


def second_kernel(attended_ref, w_ref, in_ref, vectors_ref, middle_ref, second_ref):
    groups, seqs, rows, count = attended_ref.shape
    for seq in range(seqs):
        place = pl.ds(seq * rows, rows)
        middle = in_ref[place].astype(jnp.float32) + vectors_ref[0:1]
        for group in range(groups):
            middle += dot(attended_ref[group, seq], w_ref[group * count : (group + 1) * count])
        middle_ref[place] = middle
        normal, _ = norm_parts(middle)
        second_ref[place] = (normal * vectors_ref[1:2] + vectors_ref[2:3]).astype(jnp.bfloat16)


def branch_kernel(
    own_ref, x_ref, y_ref, across_ref, grad_ref, middle_ref, vectors_ref, w_ref,
    d_middle_ref, d_branch_ref, d_attended_ref, sums_ref,
):
    groups, seqs, rows, count = d_attended_ref.shape
    d_second = total_of([own_ref[0], x_ref[...], y_ref[...], across_ref[...]])
    normal, scale = norm_parts(middle_ref[...])
    d_middle = grad_ref[...].astype(jnp.float32) + norm_back(
        normal, scale, vectors_ref[1:2], d_second
    )
    d_middle_ref[...] = d_middle
    d_branch = d_middle.astype(jnp.bfloat16)
    d_branch_ref[...] = d_branch
    for group in range(groups):
        part = dot_right(d_branch, w_ref[group * count : (group + 1) * count])
        part = part.astype(jnp.bfloat16)
        for seq in range(seqs):
            d_attended_ref[group, seq] = part[seq * rows : (seq + 1) * rows]
    sums_ref[...] = jnp.zeros_like(sums_ref)
    sums_ref[0:1] = jnp.sum(d_branch.astype(jnp.float32), 0, keepdims=True)
    sums_ref[1:2] = jnp.sum(grad_ref[...].astype(jnp.float32), 0, keepdims=True)
    sums_ref[2:3] = jnp.sum(d_second * normal, 0, keepdims=True)
    sums_ref[3:4] = jnp.sum(d_second, 0, keepdims=True)


def hidden_kernel(*refs):
    rows_refs, grad_refs = refs[:4], refs[4:8]
    w_up, w_down, bias_ref, act_ref, d_upper_ref, d_rows_ref, sums_ref = refs[8:]
    tokens = rows_refs[0].shape[0]
    skip = (grad_refs[0].shape[0] - tokens) // 2
    slope = 0.7978845608028654
    sums_ref[...] = jnp.zeros_like(sums_ref)
    for item in range(4):
        place = pl.ds(item * tokens, tokens)
        upper = dot(rows_refs[item][...], w_up[...]) + bias_ref[...]
        square = upper * upper
        bend = jnp.tanh(slope * (upper + 0.044715 * (square * upper)))
        act_ref[place] = (0.5 * upper * (1.0 + bend)).astype(jnp.bfloat16)
        rise = 0.5 * (1.0 + bend) + (0.5 * slope) * upper * (1.0 - bend * bend) * (
            1.0 + (3.0 * 0.044715) * square
        )
        d_act = dot_right(grad_refs[item][skip : skip + tokens], w_down[...])
        d_upper = (d_act * rise).astype(jnp.bfloat16)
        d_upper_ref[place] = d_upper
        sums_ref[0:1] += jnp.sum(d_upper.astype(jnp.float32), 0, keepdims=True)
        d_rows_ref[item] = dot_right(d_upper, w_up[...]).astype(jnp.bfloat16)


def hidden_weights_kernel(core_ref, *refs):
    rows_refs, grad_refs = refs[:4], refs[4:8]
    act_ref, d_upper_ref, w_down, down_ref, late_ref, up, down = refs[8:]
    tokens = rows_refs[0].shape[0]
    skip = (grad_refs[0].shape[0] - tokens) // 2
    for item in range(4):
        place = pl.ds(item * tokens, tokens)
        down_ref[item] = dot(act_ref[place], w_down[...]).astype(jnp.bfloat16)
        up_term = dot_left(rows_refs[item][...], d_upper_ref[place])
        down_term = dot_left(act_ref[place], grad_refs[item][skip : skip + tokens])
        if item == 0:
            up[...] = up_term
            down[...] = down_term
        else:
            up[...] += up_term
            down[...] += down_term
    _, columns, both, width = late_ref.shape
    half, side = both // 2, width // 2
    for order in range(2):
        start = pl.multiple_of((core_ref[0] ^ order) * side, side)
        for column in range(columns):
            top = column * both
            for part in range(2):
                late_ref[order, column, :half, part * side : (part + 1) * side] = up[
                    top + part * half : top + (part + 1) * half, pl.ds(start, side)
                ].astype(jnp.bfloat16)
            late_ref[order, column, half:] = down[
                pl.ds(pl.multiple_of(start + column * half, 8), half)
            ].astype(jnp.bfloat16)


def out_weight_kernel(place_ref, attended_ref, d_ref, grad_ref, total):
    groups, seqs, rows, count = attended_ref.shape
    for group in range(groups):
        total[group * count : (group + 1) * count] = sum(
            dot_left(attended_ref[group, seq], d_ref[seq * rows : (seq + 1) * rows])
            for seq in range(seqs)
        )
    cores, chips_count, columns, share, _ = grad_ref.shape
    plane = cores * chips_count
    for order in range(cores):
        for item in range(chips_count):
            owner = place_ref[0] ^ (2 * item + order)
            for column in range(columns):
                start = pl.multiple_of((column * plane + owner) * share, 8)
                grad_ref[order, item, column] = total[pl.ds(start, share)].astype(jnp.bfloat16)


def plane_local(
    hidden_in,
    cotangent,
    segment_ids,
    query_weight,
    key_weight,
    value_weight,
    out_weight,
    up_weight,
    down_weight,
    query_bias,
    value_bias,
    out_bias,
    up_bias,
    down_bias,
    first_gain,
    first_shift,
    second_gain,
    second_shift,
):
    seqs, rows, width = hidden_in.shape
    plane = lax.axis_size("seq")
    columns = lax.axis_size("dp")
    owners = plane * columns
    share = query_weight.shape[0]
    ff_share = down_weight.shape[0]
    hidden = up_weight.shape[1]
    group_width = width // GROUPS
    length = rows * plane
    tokens = seqs * rows
    half = plane * share // 2
    column = lax.axis_index("dp")
    place = lax.axis_index("seq")
    core, chip = place % 2, place // 2

    sent = jnp.stack([query_weight, key_weight, value_weight], 1)
    sent = sent.reshape(share, 3, GROUPS, group_width).transpose(2, 0, 1, 3)
    sent = jnp.repeat(sent.reshape(GROUPS, share, 3 * group_width), 2, axis=0)
    sent_up = up_weight.reshape(share, columns, plane, ff_share).transpose(2, 0, 1, 3)
    sent_up = sent_up.reshape(plane, share, columns * ff_share)
    sent = jnp.concatenate([sent, sent_up], -1)

    small = (
        query_bias,
        value_bias,
        out_bias,
        down_bias,
        first_gain,
        first_shift,
        second_gain,
        second_shift,
        up_bias,
        segment_ids,
    )
    sent, small, out_weight = tie(sent, small, out_weight)
    got = lax.all_to_all(sent, "seq", 0, 0, tiled=True).reshape(plane * share, -1)
    small = jnp.concatenate(small[:-1] + (small[-1].astype(jnp.bfloat16).reshape(-1),))
    small_size = small.size
    small = jnp.pad(small[None], ((0, 7), (0, width - small_size)))
    small = column_parts(jnp.concatenate([out_weight, small]), columns)
    mine = in_order(pick(hidden_in, core), swap(pick(hidden_in, 1 - core), CORE), core, 0)
    got, small, mine = tie(got, small, mine)

    got_up = got[:, 3 * group_width :]
    later = [
        got_up[:half],
        got_up[half:],
        down_weight,
        pick(got[:, : 3 * group_width].reshape(2, half, -1), core),
    ]
    later = column_parts(jnp.concatenate(later, -1), columns)

    small = column_order(small, column)
    w_out = small[:, :share].reshape(columns * share, width)
    small = jnp.pad(small[:, share], ((0, -columns % 8), (0, 0)))
    small = in_order(small, swap(small, CORE), core, 0)
    mine = chips(jnp.concatenate([mine, small], 1))
    mine = chips_order(mine, chip).reshape(plane, -1, width)
    small = mine[:, rows : rows + columns].transpose(1, 0, 2)
    mine = mine[:, :rows].reshape(length, width)
    vectors = small[:, :, : 8 * share].astype(jnp.float32).reshape(owners, 8, share)
    vectors = vectors.transpose(1, 0, 2).reshape(8, width)
    bq, bv, bo, bd, gain_one, shift_one, gain_two, shift_two = [vectors[i] for i in range(8)]
    bu = small[:, :, 8 * share : 8 * share + ff_share].astype(jnp.float32)
    bu = pick(bu.reshape(columns, GROUPS, 2, ff_share), chip, 1).transpose(1, 0, 2).reshape(-1)
    segments = pick(small[:, :, 8 * share + ff_share : small_size], column)
    segments = pick(segments.reshape(plane, seqs, rows), core, 1).reshape(length)
    segments = segments.astype(jnp.int32)
    normal_all, _ = norm_parts(mine.astype(jnp.float32))
    normed = (normal_all * gain_one + shift_one).astype(jnp.bfloat16)
    own_columns = lambda item: lax.dynamic_slice_in_dim(item, chip * group_width, group_width)
    bias_here = jnp.concatenate([own_columns(bq), jnp.zeros((group_width,)), own_columns(bv)])

    w_out = in_order(w_out, swap(w_out, CORE), core, 0)
    mine, w_out, own_low = tie(mine, w_out, cotangent.reshape(tokens, width))
    w_out = chips(w_out)
    normed, bias_here, segments, later, w_out, own_low = tie(
        normed, bias_here, segments, later, w_out, own_low
    )
    beside = chips(own_low)
    w_qkv = column_order([item[:, 2 * width :] for item in later], column)
    w_qkv = in_order(w_qkv, swap(w_qkv, CORE), core, 1).reshape(width, 3 * group_width)
    attended, projected, kept = attend(normed, w_qkv, bias_here, segments)
    attended, beside, later, w_out = tie(attended, beside, later, w_out)
    later = column_order([item[:, : 2 * width] for item in later], column)
    later_far = swap(later, CORE)
    w_out = chips_order(w_out, chip).reshape(plane, columns, share, width)
    w_out = w_out.transpose(1, 0, 2, 3).reshape(width, width)
    attended = attended.reshape(plane, rows, group_width)
    attended = lax.all_to_all(attended, "seq", 0, 0, tiled=True)
    attended = attended.reshape(GROUPS, seqs, rows, group_width)
    block_in = hidden_in.reshape(tokens, width)
    norm_vectors = jnp.stack([bo, gain_two, shift_two] + [jnp.zeros_like(bo)] * 5)
    middle, second = run(
        second_kernel,
        (attended, w_out, block_in, norm_vectors),
        (one(tokens, width), low(tokens, width)),
        2 * tokens * width * width,
    )
    second = chips(second)
    later = in_order(later, later_far, core, 0)
    w_down = later[..., width:].reshape(width, width)
    w_up = jnp.concatenate(
        [
            later[item, ..., width // 2 * side : width // 2 * (side + 1)]
            for side in range(2)
            for item in range(2)
        ],
        -1,
    )
    w_up = w_up.reshape(columns, half, 2, width).transpose(0, 2, 1, 3).reshape(width, width)

    many = GROUPS * tokens
    act, d_upper, d_rows, d_bu = run(
        hidden_kernel,
        (*second, *beside, w_up, w_down, bu[None]),
        (low(many, width), low(many, width), low(GROUPS, tokens, width), one(8, width)),
        12 * many * width * width,
    )
    d_second = [swap(d_rows[i], mask) for i, mask in ((1, NEAR_X), (2, NEAR_Y), (3, ACROSS))]
    act, d_rows = tie(act, d_rows)
    down, late = run(
        hidden_weights_kernel,
        (*second, *beside, act, d_upper, w_down),
        (low(GROUPS, tokens, width), low(2, columns, 2 * half, width)),
        12 * many * width * width,
        [pltpu.VMEM((width, width), jnp.float32)] * 2,
        (core,),
    )
    d_second, late, down = tie(d_second, late, down)
    late = plus(late[0], swap(late[1], CORE))
    d_middle, d_branch, d_attended, sums = run(
        branch_kernel,
        (d_rows, *d_second, cotangent.reshape(tokens, width), middle, norm_vectors, w_out),
        (
            one(tokens, width),
            low(tokens, width),
            low(GROUPS, seqs, rows, group_width),
            one(8, width),
        ),
        2 * tokens * width * width,
    )
    d_attended, d_branch, late = tie(d_attended, d_branch, late)
    late = column_send(late, column, columns)
    d_attended = d_attended.reshape(plane, rows, group_width)
    d_attended = lax.all_to_all(d_attended, "seq", 0, 0, tiled=True)
    (grad_out,) = run(
        out_weight_kernel,
        (attended, d_branch),
        (low(2, GROUPS, columns, share, width),),
        2 * tokens * width * width,
        [pltpu.VMEM((width, width), jnp.float32)],
        (place,),
    )
    grad_out = plus(grad_out[0], swap(grad_out[1], CORE))
    d_attended, grad_out, down = tie(d_attended, grad_out, down)
    grad_out = [grad_out[0]] + [
        swap(grad_out[i], mask) for i, mask in ((1, NEAR_X), (2, NEAR_Y), (3, ACROSS))
    ]
    down = [down[0]] + [
        swap(down[i], mask) for i, mask in ((1, NEAR_X), (2, NEAR_Y), (3, ACROSS))
    ]
    d_attended = d_attended.reshape(length, group_width)
    grad_qkv, d_first, d_sums, d_bias = attend_back(
        chip, projected, kept, d_attended, normed, w_qkv, normal_all
    )
    grad_qkv, d_first, grad_out, late = tie(grad_qkv, d_first, grad_out, late)
    d_bias = d_bias.reshape(3, group_width)

    grad_qkv = grad_qkv.reshape(columns, 2, half, -1)
    grad_qkv = plus(pick(grad_qkv, core, 1), swap(pick(grad_qkv, 1 - core, 1), CORE))
    grad_out = total_of(grad_out).astype(jnp.bfloat16).reshape(columns, -1, 3 * group_width)
    last = column_send(jnp.concatenate([grad_qkv, grad_out], 1), column, columns)
    d_first = [d_first[0]] + [
        swap(d_first[item], mask) for item, mask in ((1, NEAR_X), (2, NEAR_Y), (3, ACROSS))
    ]

    def placed(item):
        zeros = jnp.zeros((width,), jnp.float32)
        return lax.dynamic_update_slice_in_dim(zeros, item, chip * group_width, 0)

    d_bu = d_bu[0].reshape(2, columns, 1, ff_share).transpose(1, 2, 0, 3)
    d_bu = lax.dynamic_update_slice_in_dim(
        jnp.zeros((columns, GROUPS, 2, ff_share), jnp.float32), d_bu, chip, 1
    )
    terms = [
        placed(d_bias[0]),
        placed(d_bias[2]),
        sums[0],
        sums[1],
        d_sums[0],
        d_sums[1],
        sums[2],
        sums[3],
    ]
    terms = jnp.concatenate([jnp.stack(terms).T, d_bu.reshape(width, -1)], -1)

    terms = column_send(terms.reshape(columns, plane * share, -1), column, columns)
    last, late, terms, down = tie(last, late, terms, down)
    last, late, terms = total_of(last), total_of(late), total_of(terms)
    grad_up = jnp.concatenate([late[:half, : width // 2], late[:half, width // 2 :]])
    grad_down = late[half:]
    grad_out = last[half:].reshape(share, width)
    last = last[:half].astype(jnp.bfloat16)
    last = in_order(last, swap(last, CORE), core, 0).reshape(plane * share, -1)
    coarse = lax.reduce_precision(terms, 8, 7)
    terms = jnp.concatenate([coarse, terms - coarse], -1)
    last = jnp.concatenate([last, terms.astype(jnp.bfloat16), grad_up.astype(jnp.bfloat16)], -1)
    last = lax.all_to_all(last.reshape(plane, share, -1), "seq", 0, 0, tiled=True)
    last = last.astype(jnp.float32)
    grad_up = last[..., -columns * ff_share :].reshape(plane, share, columns, ff_share)
    grad_up = grad_up.transpose(1, 2, 0, 3).reshape(share, hidden)
    terms = jnp.sum(last[..., 3 * group_width : -columns * ff_share], 0)
    terms = terms[:, : terms.shape[1] // 2] + terms[:, terms.shape[1] // 2 :]
    g_bu = terms[:, 8:].reshape(-1)
    terms = terms[:, :8].T
    g_bq, g_bv, g_bo, g_bd, g_g1, g_s1, g_g2, g_s2 = [terms[i] for i in range(8)]
    grad_qkv = last[::2, :, : 3 * group_width].reshape(GROUPS, share, 3, group_width)
    grad_qkv = grad_qkv.transpose(2, 1, 0, 3).reshape(3, share, width)

    d_first = total_of(d_first).astype(jnp.bfloat16).reshape(2, rows, width)
    d_first = in_order(pick(d_first, core), swap(pick(d_first, 1 - core), CORE), core, 0)
    d_first = d_first.reshape(tokens, width).astype(jnp.float32)
    normal_one, scale_one = norm_parts(block_in.astype(jnp.float32))
    grad_input = d_middle + norm_back(normal_one, scale_one, gain_one, d_first)
    hidden_out = (middle + total_of(down) + bd).astype(jnp.bfloat16)
    return (
        hidden_out.reshape(seqs, rows, width),
        grad_input.reshape(seqs, rows, width),
        grad_qkv[0],
        grad_qkv[1],
        grad_qkv[2],
        grad_out,
        grad_up,
        grad_down,
        g_bq,
        g_bv,
        g_bo,
        g_bu,
        g_bd,
        g_g1,
        g_s1,
        g_g2,
        g_s2,
    )


def solution(mesh):
    plane = mesh.shape["seq"] == 8 and HEADS % 4 == 0
    body = plane_local if plane else wide_local
    placed = (
        P("dp", "seq", None),
        P("dp", "seq", None),
        P("dp", "seq"),
        P(("dp", "seq"), None),
        P(("dp", "seq"), None),
        P(("dp", "seq"), None),
        P(("dp", "seq"), None),
        P(("dp", "seq"), None),
        P(("dp", "seq"), None),
        P(("dp", "seq")),
        P(("dp", "seq")),
        P(("dp", "seq")),
        P(("dp", "seq")),
        P(("dp", "seq")),
        P(("dp", "seq")),
        P(("dp", "seq")),
        P(("dp", "seq")),
        P(("dp", "seq")),
    )
    return jax.shard_map(
        body,
        mesh=mesh,
        in_specs=placed,
        out_specs=(
            P("dp", "seq", None),
            P("dp", "seq", None),
            P(("dp", "seq"), None),
            P(("dp", "seq"), None),
            P(("dp", "seq"), None),
            P(("dp", "seq"), None),
            P(("dp", "seq"), None),
            P(("dp", "seq"), None),
            P(("dp", "seq")),
            P(("dp", "seq")),
            P(("dp", "seq")),
            P(("dp", "seq")),
            P(("dp", "seq")),
            P(("dp", "seq")),
            P(("dp", "seq")),
            P(("dp", "seq")),
            P(("dp", "seq")),
        ),
        check_vma=False,
    )
```

```python
import jax
import jax.numpy as jnp
from jax import lax
from jax.experimental import pallas as pl
from jax.experimental.pallas import tpu as pltpu
from jax.sharding import PartitionSpec as P

HEADS = 12
HEAD_DIM = 64
MICRO = 2


def layer_norm(value, gain, shift):
    center = value - jnp.mean(value, -1, keepdims=True)
    spread = jnp.mean(center * center, -1, keepdims=True)
    return center * lax.rsqrt(spread + 1e-05) * gain + shift


def project(left, weight):
    return jnp.einsum("spd,de->spe", left, weight, preferred_element_type=jnp.float32)


def project_back(left, weight):
    return jnp.einsum("spe,de->spd", left, weight, preferred_element_type=jnp.float32)


def weight_term(left, right):
    return jnp.einsum("spd,spe->de", left, right, preferred_element_type=jnp.float32)


def row_total(value):
    return jnp.sum(value.astype(jnp.float32), axis=(0, 1))


def wide_local(
    hidden_in,
    cotangent,
    segment_ids,
    query_weight,
    key_weight,
    value_weight,
    out_weight,
    up_weight,
    down_weight,
    query_bias,
    value_bias,
    out_bias,
    up_bias,
    down_bias,
    first_gain,
    first_shift,
    second_gain,
    second_shift,
):
    params = (
        query_weight,
        key_weight,
        value_weight,
        out_weight,
        up_weight,
        down_weight,
        query_bias,
        value_bias,
        out_bias,
        up_bias,
        down_bias,
        first_gain,
        first_shift,
        second_gain,
        second_shift,
    )
    local_seqs, shard_rows, model_width = hidden_in.shape
    group_size = local_seqs // MICRO
    owners = lax.axis_size("dp") * lax.axis_size("seq")
    seg_all = lax.all_gather(segment_ids, "seq", axis=1, tiled=True)
    query_pos = lax.axis_index("seq") * shard_rows + jnp.arange(shard_rows)
    totals = tuple(
        (jnp.zeros((item.shape[0] * owners,) + item.shape[1:], jnp.float32) for item in params)
    )
    outs_rows = []
    outs_grads = []
    for micro_step in range(MICRO):
        lower = micro_step * group_size
        upper_end = lower + group_size
        gathered = (
            lax.all_gather(params[0], ("dp", "seq"), axis=0, tiled=True),
            lax.all_gather(params[1], ("dp", "seq"), axis=0, tiled=True),
            lax.all_gather(params[2], ("dp", "seq"), axis=0, tiled=True),
            lax.all_gather(params[3], ("dp", "seq"), axis=0, tiled=True),
            lax.all_gather(params[4], ("dp", "seq"), axis=0, tiled=True),
            lax.all_gather(params[5], ("dp", "seq"), axis=0, tiled=True),
            lax.all_gather(params[6], ("dp", "seq"), axis=0, tiled=True),
            lax.all_gather(params[7], ("dp", "seq"), axis=0, tiled=True),
            lax.all_gather(params[8], ("dp", "seq"), axis=0, tiled=True),
            lax.all_gather(params[9], ("dp", "seq"), axis=0, tiled=True),
            lax.all_gather(params[10], ("dp", "seq"), axis=0, tiled=True),
            lax.all_gather(params[11], ("dp", "seq"), axis=0, tiled=True),
            lax.all_gather(params[12], ("dp", "seq"), axis=0, tiled=True),
            lax.all_gather(params[13], ("dp", "seq"), axis=0, tiled=True),
            lax.all_gather(params[14], ("dp", "seq"), axis=0, tiled=True),
        )
        wq, wk, wv, wo, wu, wd = gathered[:6]
        bq, bv, bo, bu, bd, gain_one, shift_one, gain_two, shift_two = tuple(
            (item.astype(jnp.float32) for item in gathered[6:])
        )
        block_in = hidden_in[lower:upper_end].astype(jnp.float32)
        seg_here = segment_ids[lower:upper_end]
        seg_keys = seg_all[lower:upper_end]
        normed_low = layer_norm(block_in, gain_one, shift_one).astype(jnp.bfloat16)
        queries = (
            ((project(normed_low, wq) + bq) * 0.125)
            .astype(jnp.bfloat16)
            .reshape(group_size, shard_rows, HEADS, HEAD_DIM)
        )
        key_rows = project(normed_low, wk).astype(jnp.bfloat16)
        value_rows = (project(normed_low, wv) + bv).astype(jnp.bfloat16)

        def masked_scores(key_heads):
            count_keys = key_heads.shape[1]
            raw_scores = jnp.einsum(
                "sqhd,skhd->shqk", queries, key_heads, preferred_element_type=jnp.float32
            )
            key_pos = jnp.arange(count_keys)
            same_doc = seg_here[:, :, None] == seg_keys[:, None, :]
            causal = key_pos[None, :] <= query_pos[:, None]
            allowed = (same_doc & causal[None])[:, None]
            return jnp.where(allowed, raw_scores, -1000000000.0)

        pieces = (
            lax.all_gather(key_rows, "seq", axis=1, tiled=True),
            lax.all_gather(value_rows, "seq", axis=1, tiled=True),
        )
        run_max = jnp.full((group_size, HEADS, shard_rows), -1e30, jnp.float32)
        forward_count_keys = pieces[0].shape[1]
        forward_key_heads = pieces[0].reshape(group_size, forward_count_keys, HEADS, HEAD_DIM)
        value_heads = pieces[1].reshape(group_size, forward_count_keys, HEADS, HEAD_DIM)
        forward_raw_scores = masked_scores(forward_key_heads)
        new_max = jnp.maximum(run_max, jnp.max(forward_raw_scores, -1))
        expo = jnp.exp(forward_raw_scores - new_max[..., None])
        run_sum = jnp.sum(expo, -1)
        run_acc = jnp.einsum(
            "shqk,skhd->shqd",
            expo.astype(jnp.bfloat16),
            value_heads,
            preferred_element_type=jnp.float32,
        )
        run_max, run_sum, run_acc = (new_max, run_sum, run_acc)
        attended_full = (run_acc / run_sum[..., None]).transpose(0, 2, 1, 3)
        log_total = run_max + jnp.log(run_sum)
        attended_low = attended_full.reshape(group_size, shard_rows, model_width).astype(
            jnp.bfloat16
        )
        middle = block_in + project(attended_low, wo) + bo
        second_low = layer_norm(middle, gain_two, shift_two).astype(jnp.bfloat16)
        upper_pre = project(second_low, wu) + bu
        act_full, act_back = jax.vjp(jax.nn.gelu, upper_pre)
        act_low = act_full.astype(jnp.bfloat16)
        output_rows = middle + project(act_low, wd) + bd
        outs_rows.append(output_rows.astype(jnp.bfloat16))
        grad_out = cotangent[lower:upper_end].astype(jnp.float32)
        grad_low = grad_out.astype(jnp.bfloat16)
        d_act = project_back(grad_low, wd)
        d_upper = act_back(d_act)[0].astype(jnp.bfloat16)
        d_second = project_back(d_upper, wu)
        second_norm_back = jax.vjp(layer_norm, middle, gain_two, shift_two)[1]
        d_middle_part, d_gain_two, d_shift_two = second_norm_back(d_second)
        d_middle = grad_out + d_middle_part
        d_branch = d_middle.astype(jnp.bfloat16)
        d_attended = (
            project_back(d_branch, wo)
            .astype(jnp.bfloat16)
            .reshape(group_size, shard_rows, HEADS, HEAD_DIM)
        )
        row_dots = jnp.sum(d_attended.astype(jnp.float32) * attended_full, -1).transpose(0, 2, 1)
        backward_pieces = pieces
        backward_count_keys = backward_pieces[0].shape[1]
        backward_key_heads = backward_pieces[0].reshape(
            group_size, backward_count_keys, HEADS, HEAD_DIM
        )
        backward_value_heads = backward_pieces[1].reshape(
            group_size, backward_count_keys, HEADS, HEAD_DIM
        )
        probs = jnp.exp(masked_scores(backward_key_heads) - log_total[..., None])
        d_probs = jnp.einsum(
            "sqhd,skhd->shqk", d_attended, backward_value_heads, preferred_element_type=jnp.float32
        )
        d_scores = (probs * (d_probs - row_dots[..., None])).astype(jnp.bfloat16)
        value_term = jnp.einsum(
            "shqk,sqhd->skhd",
            probs.astype(jnp.bfloat16),
            d_attended,
            preferred_element_type=jnp.float32,
        )
        key_term = jnp.einsum(
            "shqk,sqhd->skhd", d_scores, queries, preferred_element_type=jnp.float32
        )
        d_query = jnp.einsum(
            "shqk,skhd->sqhd", d_scores, backward_key_heads, preferred_element_type=jnp.float32
        )
        d_keys_all = key_term.reshape(group_size, backward_count_keys, model_width)
        d_values_all = value_term.reshape(group_size, backward_count_keys, model_width)
        d_query, d_keys_all, d_values_all = (d_query, d_keys_all, d_values_all)
        d_keys, d_values = (
            lax.psum_scatter(
                d_keys_all.astype(jnp.bfloat16), "seq", scatter_dimension=1, tiled=True
            ).astype(jnp.float32),
            lax.psum_scatter(
                d_values_all.astype(jnp.bfloat16), "seq", scatter_dimension=1, tiled=True
            ).astype(jnp.float32),
        )
        d_query_low = d_query.reshape(group_size, shard_rows, model_width).astype(jnp.bfloat16)
        d_keys_low = d_keys.astype(jnp.bfloat16)
        d_values_low = d_values.astype(jnp.bfloat16)
        d_first = (
            0.125 * project_back(d_query_low, wq)
            + project_back(d_keys_low, wk)
            + project_back(d_values_low, wv)
        )
        first_norm_back = jax.vjp(layer_norm, block_in, gain_one, shift_one)[1]
        d_input_part, d_gain_one, d_shift_one = first_norm_back(d_first)
        outs_grads.append(d_middle + d_input_part)
        grad_terms = (
            0.125 * weight_term(normed_low, d_query_low),
            weight_term(normed_low, d_keys_low),
            weight_term(normed_low, d_values_low),
            weight_term(attended_low, d_branch),
            weight_term(second_low, d_upper),
            weight_term(act_low, grad_low),
            0.125 * row_total(d_query_low),
            row_total(d_values_low),
            row_total(d_branch),
            row_total(d_upper),
            row_total(grad_low),
            d_gain_one,
            d_shift_one,
            d_gain_two,
            d_shift_two,
        )
        totals = tuple((left + right for left, right in zip(totals, grad_terms)))
    grads = lax.psum_scatter(totals, ("dp", "seq"), scatter_dimension=0, tiled=True)
    return (jnp.concatenate(outs_rows, 0), jnp.concatenate(outs_grads, 0)) + tuple(grads)


CORE, NEAR_X, NEAR_Y, ACROSS = 1, 2, 4, 6
GROUPS = 4


def tie(*values):
    return lax.optimization_barrier(values)


def swap(value, mask):
    return lax.ppermute(value, "seq", [(item, item ^ mask) for item in range(8)])


def pick(value, index, axis=0):
    return lax.dynamic_index_in_dim(value, index, axis, keepdims=False)


def in_order(own, other, bit, axis):
    return jnp.where(
        bit == 0, jnp.stack([own, other], axis), jnp.stack([other, own], axis)
    )


def plus(left, right):
    return (left.astype(jnp.float32) + right.astype(jnp.float32)).astype(jnp.bfloat16)


def total_of(parts):
    return sum(part.astype(jnp.float32) for part in parts)


def chips(value):
    return [value] + [swap(value, mask) for mask in (NEAR_X, NEAR_Y, ACROSS)]


def chips_send(order):
    got = [order(0)]
    for item, mask in ((1, NEAR_X), (2, NEAR_Y), (3, ACROSS)):
        got.append(swap(order(item), mask))
    return got


def chips_order(parts, chip):
    parts = jnp.stack(parts)
    return jnp.stack([pick(parts, chip ^ item) for item in range(GROUPS)])


def column_parts(value, count):
    parts = [value]
    for shift in range(1, count):
        perm = [(item, (item + shift) % count) for item in range(count)]
        parts.append(lax.ppermute(value, "dp", perm))
    return parts


def column_order(parts, place):
    count = len(parts)
    parts = jnp.stack(parts)
    return jnp.stack([pick(parts, (place - item) % count) for item in range(count)])


def column_send(value, place, count):
    parts = [pick(value, place)]
    for shift in range(1, count):
        sent = pick(value, (place + shift) % count)
        perm = [(item, (item + shift) % count) for item in range(count)]
        parts.append(lax.ppermute(sent, "dp", perm))
    return parts


def norm_parts(value):
    center = value - jnp.mean(value, -1, keepdims=True)
    spread_rows = jnp.mean(center * center, -1, keepdims=True)
    scale = lax.rsqrt(spread_rows + 1e-05)
    return center * scale, scale


def norm_back(normal, scale, gain, grad):
    through = grad * gain
    kept = through - jnp.mean(through, -1, keepdims=True)
    kept = kept - normal * jnp.mean(through * normal, -1, keepdims=True)
    return scale * kept


def dot(left, right):
    return jnp.dot(left, right, preferred_element_type=jnp.float32)


def dot_right(left, right):
    return lax.dot_general(
        left, right, (((1,), (1,)), ((), ())), preferred_element_type=jnp.float32
    )


def dot_left(left, right):
    return lax.dot_general(
        left, right, (((0,), (0,)), ((), ())), preferred_element_type=jnp.float32
    )


BLOCK = 256
VMEM_BYTES = 60 * 1024 * 1024


def head_mask(head, count):
    lane = lax.broadcasted_iota(jnp.int32, (1, count), 1)
    inside = (lane >= head * HEAD_DIM) & (lane < (head + 1) * HEAD_DIM)
    return inside.astype(jnp.float32).astype(jnp.bfloat16)


def head_rows(head):
    return pl.ds(pl.multiple_of(head * HEAD_DIM, HEAD_DIM), HEAD_DIM)


def flipped(value):
    return value.astype(jnp.float32).T.astype(jnp.bfloat16)


def attend_kernel(
    place_ref, own_ref, x_ref, y_ref, across_ref, w_near, w_far, vectors_ref, bias_ref, row_ref,
    normal_ref, normed_ref, w_ref, q_ref, k_ref, v_ref, full_ref, out_ref, p_ref,
    v_flip, held, column_ref,
):
    head = pl.program_id(0)
    length, count = q_ref.shape

    @pl.when(head == 0)
    def first():
        chip, core, column = place_ref[0] // 2, place_ref[0] % 2, place_ref[1]
        rows = out_ref.shape[2]
        for item, mine in enumerate((own_ref, x_ref, y_ref, across_ref)):
            for side in range(2):
                place = pl.ds(pl.multiple_of((2 * (chip ^ item) + side) * rows, rows), rows)
                normal, _ = norm_parts(mine[side, :rows].astype(jnp.float32))
                normal_ref[place] = normal.astype(jnp.bfloat16)
                normed = normal * vectors_ref[0:1] + vectors_ref[1:2]
                normed_ref[place] = normed.astype(jnp.bfloat16)
        columns, half, _ = w_near.shape
        for shift in range(columns):
            top = lax.rem(column - shift + columns, columns) * 2
            w_ref[pl.ds(pl.multiple_of((top + core) * half, 16), half)] = w_near[shift]
            w_ref[pl.ds(pl.multiple_of((top + 1 - core) * half, 16), half)] = w_far[shift]
        column_ref[...] = jnp.broadcast_to(row_ref[...], (128, length)).T
        for start in range(0, length, BLOCK):
            rows = pl.ds(start, BLOCK)
            product = dot(normed_ref[rows], w_ref[...]) + bias_ref[...]
            q_ref[rows] = (product[:, :count] * 0.125).astype(jnp.bfloat16)
            k_ref[rows] = product[:, count : 2 * count].astype(jnp.bfloat16)
            v_ref[rows] = product[:, 2 * count :].astype(jnp.bfloat16)
        v_flip[...] = flipped(v_ref[...])

    mask = head_mask(head, count)
    for start in range(0, length, BLOCK):
        stop = start + BLOCK
        scores = dot_right(k_ref[:stop], q_ref[start:stop] * mask)
        shape = (stop, BLOCK)
        causal = lax.broadcasted_iota(jnp.int32, shape, 0) <= start + lax.broadcasted_iota(
            jnp.int32, shape, 1
        )
        same = column_ref[:stop, 0:1] == row_ref[:, start:stop]
        scores = jnp.where(causal & same, scores, -1000000000.0)
        expo = jnp.exp(scores - jnp.max(scores, 0, keepdims=True))
        probs = (expo * (1.0 / jnp.sum(expo, 0, keepdims=True))).astype(jnp.bfloat16)
        p_ref[0, :stop, start:stop] = probs
        held[head_rows(head), start:stop] = dot(v_flip[head_rows(head), :stop], probs)

    @pl.when(head == pl.num_programs(0) - 1)
    def last():
        full_ref[...] = held[...]
        blocks, _, rows = out_ref.shape
        for block in range(blocks):
            out_ref[block] = held[:, block * rows : (block + 1) * rows].astype(jnp.bfloat16)


def attend_back_kernel(
    chip_ref, q_ref, k_ref, v_ref, d_ref, full_ref, normed_ref, w_ref, normal_ref, terms_in, p_ref,
    near_ref, far_ref, first_0, first_1, first_2, first_3, terms_ref,
    k_flip, dots, dq, dk, dv, d_all, d_held, grad,
):
    head = pl.program_id(0)
    length, count = q_ref.shape

    @pl.when(head == 0)
    def first():
        k_flip[...] = flipped(k_ref[...])
        blocks, _, rows = d_ref.shape
        for block in range(blocks):
            place = pl.ds(block * rows, rows)
            d_out = d_ref[block].astype(jnp.float32)
            d_held[place] = d_out.T.astype(jnp.bfloat16)
            dots[:, place] = d_out * full_ref[:, place]
        dk[...] = jnp.zeros_like(dk)
        dv[...] = jnp.zeros_like(dv)

    mask = head_mask(head, count)
    for start in range(0, length, BLOCK):
        stop = start + BLOCK
        d_out = d_held[start:stop] * mask
        probs = p_ref[0, :stop, start:stop]
        row_dots = jnp.sum(dots[head_rows(head), start:stop], 0, keepdims=True)
        d_probs = dot_right(v_ref[:stop], d_out)
        d_scores = (probs.astype(jnp.float32) * (d_probs - row_dots)).astype(jnp.bfloat16)
        dv[:stop] += dot(probs, d_out)
        dk[:stop] += dot(d_scores, q_ref[start:stop] * mask)
        dq[head_rows(head), start:stop] = dot(k_flip[head_rows(head), :stop], d_scores)

    @pl.when(head == pl.num_programs(0) - 1)
    def last():
        for start in range(0, length, BLOCK):
            rows = pl.ds(start, BLOCK)
            d_queries = dq[:, start : start + BLOCK].T.astype(jnp.bfloat16).astype(jnp.float32)
            d_all[rows] = jnp.concatenate([d_queries * 0.125, dk[rows], dv[rows]], 1).astype(
                jnp.bfloat16
            )
        width = normed_ref.shape[1]
        lane = lax.broadcasted_iota(jnp.int32, (1, width), 1) - chip_ref[0] * count
        inside = ((lane >= 0) & (lane < count)).astype(jnp.float32)
        bias = jnp.sum(d_all[...].astype(jnp.float32), 0, keepdims=True)
        bias = [
            jnp.concatenate([bias[:, item * count : (item + 1) * count]] * GROUPS, 1) * inside
            for item in (0, 2)
        ]
        grad[...] = dot_left(normed_ref[...], d_all[...])
        columns, half, _ = near_ref.shape
        for column in range(columns):
            for order, part_ref in enumerate((near_ref, far_ref)):
                start = pl.multiple_of((2 * column + (chip_ref[1] ^ order)) * half, half)
                part_ref[column] = grad[pl.ds(start, half)].astype(jnp.bfloat16)
        gain = shift = jnp.zeros((1, width), jnp.float32)
        for item in range(GROUPS):
            size = length // GROUPS
            rows = pl.ds(pl.multiple_of((chip_ref[0] ^ item) * size, size), size)
            d_first = dot_right(d_all[rows], w_ref[...])
            gain += jnp.sum(d_first * normal_ref[rows].astype(jnp.float32), 0, keepdims=True)
            shift += jnp.sum(d_first, 0, keepdims=True)
            (first_0, first_1, first_2, first_3)[item][...] = d_first.astype(jnp.bfloat16)
        row = lax.broadcasted_iota(jnp.int32, (16, 1), 0)
        terms = terms_in[...]
        for item, value in ((0, bias[0]), (1, bias[1]), (4, gain), (5, shift)):
            terms = jnp.where(row == item, value, terms)
        coarse = terms.astype(jnp.bfloat16).astype(jnp.float32)
        fine = terms - coarse
        columns = terms_ref.shape[0]
        size = width // columns
        for column in range(columns):
            part = slice(column * size, (column + 1) * size)
            terms_ref[column] = jnp.concatenate(
                [coarse[:, part], fine[:, part], jnp.zeros((16, count * 3 - 2 * size), jnp.float32)], 1
            ).astype(jnp.bfloat16)


def whole(*shape):
    return pl.BlockSpec(shape, lambda head: (0,) * len(shape))


def kernel_params():
    return pltpu.CompilerParams(
        dimension_semantics=("arbitrary",), vmem_limit_bytes=VMEM_BYTES
    )


def attend(place, column, mine, near, far, vectors, bias, segments):
    _, padded, width = mine[0].shape
    columns, half, _ = near.shape
    length = segments.shape[0]
    count = near.shape[2] // 3
    heads = count // HEAD_DIM
    shape = (length, count)
    blocks = (2 * GROUPS, count, length // (2 * GROUPS))
    probs = pl.BlockSpec((1, length, length), lambda head: (head, 0, 0))
    normal, normed, weights, queries, keys, values, full, out, probs = pl.pallas_call(
        attend_kernel,
        grid=(heads,),
        in_specs=[pl.BlockSpec(memory_space=pltpu.SMEM)]
        + [whole(2, padded, width)] * 4
        + [whole(*near.shape)] * 2
        + [whole(8, width), whole(1, 3 * count), whole(1, length)],
        out_specs=[whole(length, width)] * 2
        + [whole(width, 3 * count)]
        + [whole(*shape)] * 3
        + [whole(count, length), whole(*blocks), probs],
        out_shape=[
            low(length, width),
            low(length, width),
            low(width, 3 * count),
            low(*shape),
            low(*shape),
            low(*shape),
            one(count, length),
            low(*blocks),
            low(heads, length, length),
        ],
        scratch_shapes=[
            pltpu.VMEM((count, length), jnp.bfloat16),
            pltpu.VMEM((count, length), jnp.float32),
            pltpu.VMEM((length, 128), jnp.float32),
        ],
        compiler_params=kernel_params(),
        cost_estimate=pl.CostEstimate(
            flops=4 * length * length * count + 6 * length * width * count,
            bytes_accessed=2 * heads * length * length,
            transcendentals=heads * length * length,
        ),
    )(jnp.stack([place, column]), *mine, near, far, vectors, bias[None], segments[None])
    return out, (queries, keys, values), (full, probs), (normal, normed, weights)


def attend_back(place, columns, projected, kept, d_out, normed, weights, normal, terms):
    length, width = normed.shape
    count = d_out.shape[1]
    heads = count // HEAD_DIM
    shape = (length, count)
    full, probs = kept
    size = length // GROUPS
    return pl.pallas_call(
        attend_back_kernel,
        grid=(heads,),
        in_specs=[pl.BlockSpec(memory_space=pltpu.SMEM)]
        + [whole(*shape)] * 3
        + [
            whole(*d_out.shape),
            whole(count, length),
            whole(length, width),
            whole(width, 3 * count),
            whole(length, width),
            whole(16, width),
            pl.BlockSpec((1, length, length), lambda head: (head, 0, 0)),
        ],
        out_specs=[
            whole(columns, width // columns // 2, 3 * count),
            whole(columns, width // columns // 2, 3 * count),
            whole(size, width),
            whole(size, width),
            whole(size, width),
            whole(size, width),
            whole(columns, 16, 3 * count),
        ],
        out_shape=[
            low(columns, width // columns // 2, 3 * count),
            low(columns, width // columns // 2, 3 * count),
            low(size, width),
            low(size, width),
            low(size, width),
            low(size, width),
            low(columns, 16, 3 * count),
        ],
        scratch_shapes=[
            pltpu.VMEM((count, length), jnp.bfloat16),
            pltpu.VMEM((count, length), jnp.float32),
            pltpu.VMEM((count, length), jnp.float32),
            pltpu.VMEM(shape, jnp.float32),
            pltpu.VMEM(shape, jnp.float32),
            pltpu.VMEM((length, 3 * count), jnp.bfloat16),
            pltpu.VMEM(shape, jnp.bfloat16),
            pltpu.VMEM((width, 3 * count), jnp.float32),
        ],
        compiler_params=kernel_params(),
        cost_estimate=pl.CostEstimate(
            flops=10 * length * length * count + 12 * length * width * count,
            bytes_accessed=2 * heads * length * length,
            transcendentals=0,
        ),
    )(jnp.stack([place // 2, place % 2]), *projected, d_out, full, normed, weights, normal, terms, probs)


def one(*shape):
    return jax.ShapeDtypeStruct(shape, jnp.float32)


def low(*shape):
    return jax.ShapeDtypeStruct(shape, jnp.bfloat16)


def run(body, given, outs, flops, scratch=(), scalars=()):
    specs = [pl.BlockSpec(memory_space=pltpu.SMEM)] * len(scalars)
    return pl.pallas_call(
        body,
        grid=(1,),
        in_specs=specs + [whole(*item.shape) for item in given],
        out_specs=[whole(*item.shape) for item in outs],
        out_shape=list(outs),
        scratch_shapes=list(scratch),
        compiler_params=pltpu.CompilerParams(vmem_limit_bytes=VMEM_BYTES),
        cost_estimate=pl.CostEstimate(flops=flops, bytes_accessed=0, transcendentals=0),
    )(*[item[None] for item in scalars], *given)


def second_kernel(attended_ref, w_ref, in_ref, vectors_ref, middle_ref, second_ref):
    blocks, count, rows = attended_ref.shape
    groups, seqs = blocks // 2, 2
    for seq in range(seqs):
        place = pl.ds(seq * rows, rows)
        middle = in_ref[place].astype(jnp.float32) + vectors_ref[0:1]
        for group in range(groups):
            middle += dot_left(
                attended_ref[seqs * group + seq], w_ref[group * count : (group + 1) * count]
            )
        middle_ref[place] = middle
        normal, _ = norm_parts(middle)
        second_ref[place] = (normal * vectors_ref[1:2] + vectors_ref[2:3]).astype(jnp.bfloat16)


def branch_kernel(
    place_ref, own_ref, x_ref, y_ref, across_ref, grad_ref, middle_ref, vectors_ref, w_ref,
    attended_ref, d_middle_ref, d_attended_ref, sums_ref, near_ref, far_ref, total,
):
    blocks, count, rows = d_attended_ref.shape
    groups, seqs = blocks // 2, 2
    d_second = total_of([own_ref[...], x_ref[...], y_ref[...], across_ref[...]])
    normal, scale = norm_parts(middle_ref[...])
    d_middle = grad_ref[...].astype(jnp.float32) + norm_back(
        normal, scale, vectors_ref[1:2], d_second
    )
    d_middle_ref[...] = d_middle
    d_branch = d_middle.astype(jnp.bfloat16)
    for group in range(groups):
        part = dot_right(w_ref[group * count : (group + 1) * count], d_branch)
        part = part.astype(jnp.bfloat16)
        for seq in range(seqs):
            d_attended_ref[seqs * group + seq] = part[:, seq * rows : (seq + 1) * rows]
        total[group * count : (group + 1) * count] = sum(
            dot(attended_ref[seqs * group + seq], d_branch[seq * rows : (seq + 1) * rows])
            for seq in range(seqs)
        )
    chips_count, columns, share, _ = near_ref.shape
    for order, grad_out_ref in enumerate((near_ref, far_ref)):
        for item in range(chips_count):
            owner = place_ref[0] ^ (2 * item + order)
            for column in range(columns):
                start = pl.multiple_of((column * blocks + owner) * share, 8)
                grad_out_ref[item, column] = total[pl.ds(start, share)].astype(jnp.bfloat16)
    sums_ref[...] = jnp.zeros_like(sums_ref)
    sums_ref[0:1] = jnp.sum(d_branch.astype(jnp.float32), 0, keepdims=True)
    sums_ref[1:2] = jnp.sum(grad_ref[...].astype(jnp.float32), 0, keepdims=True)
    sums_ref[2:3] = jnp.sum(d_second * normal, 0, keepdims=True)
    sums_ref[3:4] = jnp.sum(d_second, 0, keepdims=True)


def hidden_kernel(*refs):
    rows_refs, grad_refs = refs[:4], refs[4:8]
    w_up, w_down, bias_ref, act_ref, d_upper_ref, *d_rows_refs, sums_ref = refs[8:]
    tokens = rows_refs[0].shape[0]
    skip = (grad_refs[0].shape[0] - tokens) // 2
    slope = 0.7978845608028654
    sums_ref[...] = jnp.zeros_like(sums_ref)
    for item in range(4):
        place = pl.ds(item * tokens, tokens)
        upper = dot(rows_refs[item][...], w_up[...]) + bias_ref[...]
        square = upper * upper
        bend = jnp.tanh(slope * (upper + 0.044715 * (square * upper)))
        act_ref[place] = (0.5 * upper * (1.0 + bend)).astype(jnp.bfloat16)
        rise = 0.5 * (1.0 + bend) + (0.5 * slope) * upper * (1.0 - bend * bend) * (
            1.0 + (3.0 * 0.044715) * square
        )
        d_act = dot_right(grad_refs[item][skip : skip + tokens], w_down[...])
        d_upper = (d_act * rise).astype(jnp.bfloat16)
        d_upper_ref[place] = d_upper
        sums_ref[0:1] += jnp.sum(d_upper.astype(jnp.float32), 0, keepdims=True)
        d_rows_refs[item][...] = dot_right(d_upper, w_up[...]).astype(jnp.bfloat16)


def hidden_weights_kernel(core_ref, *refs):
    rows_refs, grad_refs = refs[:4], refs[4:8]
    act_ref, d_upper_ref, w_down, *down_refs, late_near, late_far, up, down = refs[8:]
    tokens = rows_refs[0].shape[0]
    skip = (grad_refs[0].shape[0] - tokens) // 2
    for item in range(4):
        place = pl.ds(item * tokens, tokens)
        down_refs[item][...] = dot(act_ref[place], w_down[...]).astype(jnp.bfloat16)
        up_term = dot_left(rows_refs[item][...], d_upper_ref[place])
        down_term = dot_left(act_ref[place], grad_refs[item][skip : skip + tokens])
        if item == 0:
            up[...] = up_term
            down[...] = down_term
        else:
            up[...] += up_term
            down[...] += down_term
    columns, both, width = late_near.shape
    half, side = both // 2, width // 2
    for order in range(2):
        late_ref = (late_near, late_far)[order]
        start = pl.multiple_of((core_ref[0] ^ order) * side, side)
        for column in range(columns):
            top = column * both
            for part in range(2):
                late_ref[column, :half, part * side : (part + 1) * side] = up[
                    top + part * half : top + (part + 1) * half, pl.ds(start, side)
                ].astype(jnp.bfloat16)
            late_ref[column, half:] = down[
                pl.ds(pl.multiple_of(start + column * half, 8), half)
            ].astype(jnp.bfloat16)


def plane_local(
    hidden_in,
    cotangent,
    segment_ids,
    query_weight,
    key_weight,
    value_weight,
    out_weight,
    up_weight,
    down_weight,
    query_bias,
    value_bias,
    out_bias,
    up_bias,
    down_bias,
    first_gain,
    first_shift,
    second_gain,
    second_shift,
):
    seqs, rows, width = hidden_in.shape
    plane = lax.axis_size("seq")
    columns = lax.axis_size("dp")
    owners = plane * columns
    share = query_weight.shape[0]
    ff_share = down_weight.shape[0]
    hidden = up_weight.shape[1]
    group_width = width // GROUPS
    length = rows * plane
    tokens = seqs * rows
    half = plane * share // 2
    column = lax.axis_index("dp")
    place = lax.axis_index("seq")
    core, chip = place % 2, place // 2

    sent = jnp.stack([query_weight, key_weight, value_weight], 1)
    sent = sent.reshape(share, 3, GROUPS, group_width).transpose(2, 0, 1, 3)
    sent = jnp.repeat(sent.reshape(GROUPS, share, 3 * group_width), 2, axis=0)
    sent_up = up_weight.reshape(share, columns, plane, ff_share).transpose(2, 0, 1, 3)
    sent_up = sent_up.reshape(plane, share, columns * ff_share)
    sent = jnp.concatenate([sent, sent_up], -1)

    small = (
        query_bias,
        value_bias,
        out_bias,
        down_bias,
        first_gain,
        first_shift,
        second_gain,
        second_shift,
        up_bias,
        segment_ids,
    )
    sent, small, out_weight = tie(sent, small, out_weight)
    got = lax.all_to_all(sent, "seq", 0, 0, tiled=True).reshape(plane * share, -1)
    small = jnp.concatenate(small[:-1] + (small[-1].astype(jnp.bfloat16).reshape(-1),))
    small_size = small.size
    small = jnp.pad(small[None], ((0, 7), (0, width - small_size)))
    small = column_parts(jnp.concatenate([out_weight, small]), columns)
    mine = in_order(pick(hidden_in, core), swap(pick(hidden_in, 1 - core), CORE), core, 0)
    got, small, mine = tie(got, small, mine)

    got_up = got[:, 3 * group_width :]
    later = [
        got_up[:half],
        got_up[half:],
        down_weight,
        pick(got[:, : 3 * group_width].reshape(2, half, -1), core),
    ]
    later = column_parts(jnp.concatenate(later, -1), columns)

    small = column_order(small, column)
    w_out = small[:, :share].reshape(columns * share, width)
    small = jnp.pad(small[:, share], ((0, -columns % 8), (0, 0)))
    small = in_order(small, swap(small, CORE), core, 0)
    mine = chips(jnp.concatenate([mine, small], 1))
    small = chips_order([item[:, rows : rows + columns] for item in mine], chip)
    small = small.reshape(plane, columns, width).transpose(1, 0, 2)
    vectors = small[:, :, : 8 * share].astype(jnp.float32).reshape(owners, 8, share)
    vectors = vectors.transpose(1, 0, 2).reshape(8, width)
    bq, bv, bo, bd, gain_one, shift_one, gain_two, shift_two = [vectors[i] for i in range(8)]
    bu = small[:, :, 8 * share : 8 * share + ff_share].astype(jnp.float32)
    bu = pick(bu.reshape(columns, GROUPS, 2, ff_share), chip, 1).transpose(1, 0, 2).reshape(-1)
    segments = pick(small[:, :, 8 * share + ff_share : small_size], column)
    segments = pick(segments.reshape(plane, seqs, rows), core, 1).reshape(length)
    segments = segments.astype(jnp.float32)
    first_vectors = jnp.stack([gain_one, shift_one] + [jnp.zeros_like(bo)] * 6)
    own_columns = lambda item: lax.dynamic_slice_in_dim(item, chip * group_width, group_width)
    bias_here = jnp.concatenate([own_columns(bq), jnp.zeros((group_width,)), own_columns(bv)])

    w_out = in_order(w_out, swap(w_out, CORE), core, 0)
    mine, w_out, own_low = tie(mine, w_out, cotangent.reshape(tokens, width))
    w_out = chips(w_out)
    first_vectors, bias_here, segments, later, w_out, own_low = tie(
        first_vectors, bias_here, segments, later, w_out, own_low
    )
    beside = chips(own_low)
    w_qkv = jnp.stack([item[:, 2 * width :] for item in later])
    attended, projected, kept, (normal_all, normed, w_qkv) = attend(
        place, column, mine, w_qkv, swap(w_qkv, CORE), first_vectors, bias_here, segments
    )
    attended, beside, later, w_out = tie(attended, beside, later, w_out)
    later = column_order([item[:, : 2 * width] for item in later], column)
    later_far = swap(later, CORE)
    w_out = chips_order(w_out, chip).reshape(plane, columns, share, width)
    w_out = w_out.transpose(1, 0, 2, 3).reshape(width, width)
    attended = lax.all_to_all(attended, "seq", 0, 0, tiled=True)
    block_in = hidden_in.reshape(tokens, width)
    norm_vectors = jnp.stack([bo, gain_two, shift_two] + [jnp.zeros_like(bo)] * 5)
    middle, second = run(
        second_kernel,
        (attended, w_out, block_in, norm_vectors),
        (one(tokens, width), low(tokens, width)),
        2 * tokens * width * width,
    )
    second = chips(second)
    later = in_order(later, later_far, core, 0)
    w_down = later[..., width:].reshape(width, width)
    w_up = jnp.concatenate(
        [
            later[item, ..., width // 2 * side : width // 2 * (side + 1)]
            for side in range(2)
            for item in range(2)
        ],
        -1,
    )
    w_up = w_up.reshape(columns, half, 2, width).transpose(0, 2, 1, 3).reshape(width, width)

    many = GROUPS * tokens
    act, d_upper, *d_rows, d_bu = run(
        hidden_kernel,
        (*second, *beside, w_up, w_down, bu[None]),
        (low(many, width), low(many, width), *[low(tokens, width)] * 4, one(8, width)),
        12 * many * width * width,
    )
    d_second = [swap(d_rows[i], mask) for i, mask in ((1, NEAR_X), (2, NEAR_Y), (3, ACROSS))]
    act, d_rows = tie(act, d_rows)
    *down, late, late_far = run(
        hidden_weights_kernel,
        (*second, *beside, act, d_upper, w_down),
        (*[low(tokens, width)] * 4, *[low(columns, 2 * half, width)] * 2),
        12 * many * width * width,
        [pltpu.VMEM((width, width), jnp.float32)] * 2,
        (core,),
    )
    d_second, late, late_far, down = tie(d_second, late, late_far, down)
    late = plus(late, swap(late_far, CORE))
    d_middle, d_attended, sums, grad_out, grad_far = run(
        branch_kernel,
        (
            d_rows[0],
            *d_second,
            cotangent.reshape(tokens, width),
            middle,
            norm_vectors,
            w_out,
            attended,
        ),
        (
            one(tokens, width),
            low(plane, group_width, rows),
            one(8, width),
            *[low(GROUPS, columns, share, width)] * 2,
        ),
        4 * tokens * width * width,
        [pltpu.VMEM((width, width), jnp.float32)],
        (place,),
    )
    d_attended, late = tie(d_attended, late)
    late = column_send(late, column, columns)
    d_attended = lax.all_to_all(d_attended, "seq", 0, 0, tiled=True)
    grad_out = plus(grad_out, swap(grad_far, CORE))
    d_attended, down, late[1] = tie(d_attended, down, late[1])
    grad_out = [grad_out[0]] + [
        swap(grad_out[i], mask) for i, mask in ((1, NEAR_X), (2, NEAR_Y), (3, ACROSS))
    ]
    down = [down[0]] + [
        swap(down[i], mask) for i, mask in ((1, NEAR_X), (2, NEAR_Y), (3, ACROSS))
    ]
    d_bu = lax.dynamic_update_slice_in_dim(
        jnp.zeros((columns, GROUPS, 2, ff_share), jnp.float32),
        d_bu[0].reshape(2, columns, 1, ff_share).transpose(1, 2, 0, 3),
        chip,
        1,
    )
    d_bu = d_bu.reshape(owners, -1, share).transpose(1, 0, 2).reshape(-1, width)
    blank = jnp.zeros((2, width), jnp.float32)
    terms = jnp.concatenate([blank, sums[:2], blank, sums[2:4], d_bu, blank, blank])
    grad_near, grad_far, *d_first, terms = attend_back(
        place, columns, projected, kept, d_attended, normed, w_qkv, normal_all, terms
    )
    grad_near, grad_far, terms, grad_out, down, late = tie(
        grad_near, grad_far, terms, grad_out, down, late
    )

    grad_qkv = plus(grad_near, swap(grad_far, CORE))
    grad_out = total_of(grad_out).astype(jnp.bfloat16).reshape(columns, -1, 3 * group_width)
    last = jnp.concatenate([grad_qkv, grad_out, terms], 1)
    last = lax.all_to_all(last, "dp", 0, 0, tiled=True)
    d_first = [d_first[0]] + [
        swap(d_first[item], mask) for item, mask in ((1, NEAR_X), (2, NEAR_Y), (3, ACROSS))
    ]

    last, late, d_first = tie(last, late, d_first)
    last, late = jnp.sum(last.astype(jnp.float32), 0), total_of(late)
    grad_up = jnp.concatenate([late[:half, : width // 2], late[:half, width // 2 :]])
    grad_down = late[half:]
    grad_out = last[half:-16].reshape(share, width)
    terms = last[-16:, :group_width] + last[-16:, group_width : 2 * group_width]
    terms = terms[:12].T
    last = last[:half].astype(jnp.bfloat16)
    last = in_order(last, swap(last, CORE), core, 0).reshape(plane * share, -1)
    coarse = lax.reduce_precision(terms, 8, 7)
    terms = jnp.concatenate([coarse, terms - coarse], -1)
    last = jnp.concatenate([last, terms.astype(jnp.bfloat16), grad_up.astype(jnp.bfloat16)], -1)
    last = lax.all_to_all(last.reshape(plane, share, -1), "seq", 0, 0, tiled=True)
    last = last.astype(jnp.float32)
    grad_up = last[..., -columns * ff_share :].reshape(plane, share, columns, ff_share)
    grad_up = grad_up.transpose(1, 2, 0, 3).reshape(share, hidden)
    terms = jnp.sum(last[..., 3 * group_width : -columns * ff_share], 0)
    terms = terms[:, : terms.shape[1] // 2] + terms[:, terms.shape[1] // 2 :]
    terms = terms.T
    g_bu = terms[8:].reshape(-1)
    g_bq, g_bv, g_bo, g_bd, g_g1, g_s1, g_g2, g_s2 = [terms[i] for i in range(8)]
    grad_qkv = last[::2, :, : 3 * group_width].reshape(GROUPS, share, 3, group_width)
    grad_qkv = grad_qkv.transpose(2, 1, 0, 3).reshape(3, share, width)

    d_first = total_of(d_first).astype(jnp.bfloat16).reshape(2, rows, width)
    d_first = in_order(pick(d_first, core), swap(pick(d_first, 1 - core), CORE), core, 0)
    d_first = d_first.reshape(tokens, width).astype(jnp.float32)
    normal_one, scale_one = norm_parts(block_in.astype(jnp.float32))
    grad_input = d_middle + norm_back(normal_one, scale_one, gain_one, d_first)
    hidden_out = (middle + total_of(down) + bd).astype(jnp.bfloat16)
    return (
        hidden_out.reshape(seqs, rows, width),
        grad_input.reshape(seqs, rows, width),
        grad_qkv[0],
        grad_qkv[1],
        grad_qkv[2],
        grad_out,
        grad_up,
        grad_down,
        g_bq,
        g_bv,
        g_bo,
        g_bu,
        g_bd,
        g_g1,
        g_s1,
        g_g2,
        g_s2,
    )


def solution(mesh):
    plane = mesh.shape["seq"] == 8 and HEADS % 4 == 0
    body = plane_local if plane else wide_local
    placed = (
        P("dp", "seq", None),
        P("dp", "seq", None),
        P("dp", "seq"),
        P(("dp", "seq"), None),
        P(("dp", "seq"), None),
        P(("dp", "seq"), None),
        P(("dp", "seq"), None),
        P(("dp", "seq"), None),
        P(("dp", "seq"), None),
        P(("dp", "seq")),
        P(("dp", "seq")),
        P(("dp", "seq")),
        P(("dp", "seq")),
        P(("dp", "seq")),
        P(("dp", "seq")),
        P(("dp", "seq")),
        P(("dp", "seq")),
        P(("dp", "seq")),
    )
    return jax.shard_map(
        body,
        mesh=mesh,
        in_specs=placed,
        out_specs=(
            P("dp", "seq", None),
            P("dp", "seq", None),
            P(("dp", "seq"), None),
            P(("dp", "seq"), None),
            P(("dp", "seq"), None),
            P(("dp", "seq"), None),
            P(("dp", "seq"), None),
            P(("dp", "seq"), None),
            P(("dp", "seq")),
            P(("dp", "seq")),
            P(("dp", "seq")),
            P(("dp", "seq")),
            P(("dp", "seq")),
            P(("dp", "seq")),
            P(("dp", "seq")),
            P(("dp", "seq")),
            P(("dp", "seq")),
        ),
        check_vma=False,
    )
```

```python
import jax
import jax.numpy as jnp
from jax import lax
from jax.experimental import pallas as pl
from jax.experimental.pallas import tpu as pltpu
from jax.sharding import PartitionSpec as P

HEADS = 12
HEAD_DIM = 64
MICRO = 2


def layer_norm(value, gain, shift):
    center = value - jnp.mean(value, -1, keepdims=True)
    spread = jnp.mean(center * center, -1, keepdims=True)
    return center * lax.rsqrt(spread + 1e-05) * gain + shift


def project(left, weight):
    return jnp.einsum("spd,de->spe", left, weight, preferred_element_type=jnp.float32)


def project_back(left, weight):
    return jnp.einsum("spe,de->spd", left, weight, preferred_element_type=jnp.float32)


def weight_term(left, right):
    return jnp.einsum("spd,spe->de", left, right, preferred_element_type=jnp.float32)


def row_total(value):
    return jnp.sum(value.astype(jnp.float32), axis=(0, 1))


def wide_local(
    hidden_in,
    cotangent,
    segment_ids,
    query_weight,
    key_weight,
    value_weight,
    out_weight,
    up_weight,
    down_weight,
    query_bias,
    value_bias,
    out_bias,
    up_bias,
    down_bias,
    first_gain,
    first_shift,
    second_gain,
    second_shift,
):
    params = (
        query_weight,
        key_weight,
        value_weight,
        out_weight,
        up_weight,
        down_weight,
        query_bias,
        value_bias,
        out_bias,
        up_bias,
        down_bias,
        first_gain,
        first_shift,
        second_gain,
        second_shift,
    )
    local_seqs, shard_rows, model_width = hidden_in.shape
    group_size = local_seqs // MICRO
    owners = lax.axis_size("dp") * lax.axis_size("seq")
    seg_all = lax.all_gather(segment_ids, "seq", axis=1, tiled=True)
    query_pos = lax.axis_index("seq") * shard_rows + jnp.arange(shard_rows)
    totals = tuple(
        (jnp.zeros((item.shape[0] * owners,) + item.shape[1:], jnp.float32) for item in params)
    )
    outs_rows = []
    outs_grads = []
    for micro_step in range(MICRO):
        lower = micro_step * group_size
        upper_end = lower + group_size
        gathered = (
            lax.all_gather(params[0], ("dp", "seq"), axis=0, tiled=True),
            lax.all_gather(params[1], ("dp", "seq"), axis=0, tiled=True),
            lax.all_gather(params[2], ("dp", "seq"), axis=0, tiled=True),
            lax.all_gather(params[3], ("dp", "seq"), axis=0, tiled=True),
            lax.all_gather(params[4], ("dp", "seq"), axis=0, tiled=True),
            lax.all_gather(params[5], ("dp", "seq"), axis=0, tiled=True),
            lax.all_gather(params[6], ("dp", "seq"), axis=0, tiled=True),
            lax.all_gather(params[7], ("dp", "seq"), axis=0, tiled=True),
            lax.all_gather(params[8], ("dp", "seq"), axis=0, tiled=True),
            lax.all_gather(params[9], ("dp", "seq"), axis=0, tiled=True),
            lax.all_gather(params[10], ("dp", "seq"), axis=0, tiled=True),
            lax.all_gather(params[11], ("dp", "seq"), axis=0, tiled=True),
            lax.all_gather(params[12], ("dp", "seq"), axis=0, tiled=True),
            lax.all_gather(params[13], ("dp", "seq"), axis=0, tiled=True),
            lax.all_gather(params[14], ("dp", "seq"), axis=0, tiled=True),
        )
        wq, wk, wv, wo, wu, wd = gathered[:6]
        bq, bv, bo, bu, bd, gain_one, shift_one, gain_two, shift_two = tuple(
            (item.astype(jnp.float32) for item in gathered[6:])
        )
        block_in = hidden_in[lower:upper_end].astype(jnp.float32)
        seg_here = segment_ids[lower:upper_end]
        seg_keys = seg_all[lower:upper_end]
        normed_low = layer_norm(block_in, gain_one, shift_one).astype(jnp.bfloat16)
        queries = (
            ((project(normed_low, wq) + bq) * 0.125)
            .astype(jnp.bfloat16)
            .reshape(group_size, shard_rows, HEADS, HEAD_DIM)
        )
        key_rows = project(normed_low, wk).astype(jnp.bfloat16)
        value_rows = (project(normed_low, wv) + bv).astype(jnp.bfloat16)

        def masked_scores(key_heads):
            count_keys = key_heads.shape[1]
            raw_scores = jnp.einsum(
                "sqhd,skhd->shqk", queries, key_heads, preferred_element_type=jnp.float32
            )
            key_pos = jnp.arange(count_keys)
            same_doc = seg_here[:, :, None] == seg_keys[:, None, :]
            causal = key_pos[None, :] <= query_pos[:, None]
            allowed = (same_doc & causal[None])[:, None]
            return jnp.where(allowed, raw_scores, -1000000000.0)

        pieces = (
            lax.all_gather(key_rows, "seq", axis=1, tiled=True),
            lax.all_gather(value_rows, "seq", axis=1, tiled=True),
        )
        run_max = jnp.full((group_size, HEADS, shard_rows), -1e30, jnp.float32)
        forward_count_keys = pieces[0].shape[1]
        forward_key_heads = pieces[0].reshape(group_size, forward_count_keys, HEADS, HEAD_DIM)
        value_heads = pieces[1].reshape(group_size, forward_count_keys, HEADS, HEAD_DIM)
        forward_raw_scores = masked_scores(forward_key_heads)
        new_max = jnp.maximum(run_max, jnp.max(forward_raw_scores, -1))
        expo = jnp.exp(forward_raw_scores - new_max[..., None])
        run_sum = jnp.sum(expo, -1)
        run_acc = jnp.einsum(
            "shqk,skhd->shqd",
            expo.astype(jnp.bfloat16),
            value_heads,
            preferred_element_type=jnp.float32,
        )
        run_max, run_sum, run_acc = (new_max, run_sum, run_acc)
        attended_full = (run_acc / run_sum[..., None]).transpose(0, 2, 1, 3)
        log_total = run_max + jnp.log(run_sum)
        attended_low = attended_full.reshape(group_size, shard_rows, model_width).astype(
            jnp.bfloat16
        )
        middle = block_in + project(attended_low, wo) + bo
        second_low = layer_norm(middle, gain_two, shift_two).astype(jnp.bfloat16)
        upper_pre = project(second_low, wu) + bu
        act_full, act_back = jax.vjp(jax.nn.gelu, upper_pre)
        act_low = act_full.astype(jnp.bfloat16)
        output_rows = middle + project(act_low, wd) + bd
        outs_rows.append(output_rows.astype(jnp.bfloat16))
        grad_out = cotangent[lower:upper_end].astype(jnp.float32)
        grad_low = grad_out.astype(jnp.bfloat16)
        d_act = project_back(grad_low, wd)
        d_upper = act_back(d_act)[0].astype(jnp.bfloat16)
        d_second = project_back(d_upper, wu)
        second_norm_back = jax.vjp(layer_norm, middle, gain_two, shift_two)[1]
        d_middle_part, d_gain_two, d_shift_two = second_norm_back(d_second)
        d_middle = grad_out + d_middle_part
        d_branch = d_middle.astype(jnp.bfloat16)
        d_attended = (
            project_back(d_branch, wo)
            .astype(jnp.bfloat16)
            .reshape(group_size, shard_rows, HEADS, HEAD_DIM)
        )
        row_dots = jnp.sum(d_attended.astype(jnp.float32) * attended_full, -1).transpose(0, 2, 1)
        backward_pieces = pieces
        backward_count_keys = backward_pieces[0].shape[1]
        backward_key_heads = backward_pieces[0].reshape(
            group_size, backward_count_keys, HEADS, HEAD_DIM
        )
        backward_value_heads = backward_pieces[1].reshape(
            group_size, backward_count_keys, HEADS, HEAD_DIM
        )
        probs = jnp.exp(masked_scores(backward_key_heads) - log_total[..., None])
        d_probs = jnp.einsum(
            "sqhd,skhd->shqk", d_attended, backward_value_heads, preferred_element_type=jnp.float32
        )
        d_scores = (probs * (d_probs - row_dots[..., None])).astype(jnp.bfloat16)
        value_term = jnp.einsum(
            "shqk,sqhd->skhd",
            probs.astype(jnp.bfloat16),
            d_attended,
            preferred_element_type=jnp.float32,
        )
        key_term = jnp.einsum(
            "shqk,sqhd->skhd", d_scores, queries, preferred_element_type=jnp.float32
        )
        d_query = jnp.einsum(
            "shqk,skhd->sqhd", d_scores, backward_key_heads, preferred_element_type=jnp.float32
        )
        d_keys_all = key_term.reshape(group_size, backward_count_keys, model_width)
        d_values_all = value_term.reshape(group_size, backward_count_keys, model_width)
        d_query, d_keys_all, d_values_all = (d_query, d_keys_all, d_values_all)
        d_keys, d_values = (
            lax.psum_scatter(
                d_keys_all.astype(jnp.bfloat16), "seq", scatter_dimension=1, tiled=True
            ).astype(jnp.float32),
            lax.psum_scatter(
                d_values_all.astype(jnp.bfloat16), "seq", scatter_dimension=1, tiled=True
            ).astype(jnp.float32),
        )
        d_query_low = d_query.reshape(group_size, shard_rows, model_width).astype(jnp.bfloat16)
        d_keys_low = d_keys.astype(jnp.bfloat16)
        d_values_low = d_values.astype(jnp.bfloat16)
        d_first = (
            0.125 * project_back(d_query_low, wq)
            + project_back(d_keys_low, wk)
            + project_back(d_values_low, wv)
        )
        first_norm_back = jax.vjp(layer_norm, block_in, gain_one, shift_one)[1]
        d_input_part, d_gain_one, d_shift_one = first_norm_back(d_first)
        outs_grads.append(d_middle + d_input_part)
        grad_terms = (
            0.125 * weight_term(normed_low, d_query_low),
            weight_term(normed_low, d_keys_low),
            weight_term(normed_low, d_values_low),
            weight_term(attended_low, d_branch),
            weight_term(second_low, d_upper),
            weight_term(act_low, grad_low),
            0.125 * row_total(d_query_low),
            row_total(d_values_low),
            row_total(d_branch),
            row_total(d_upper),
            row_total(grad_low),
            d_gain_one,
            d_shift_one,
            d_gain_two,
            d_shift_two,
        )
        totals = tuple((left + right for left, right in zip(totals, grad_terms)))
    grads = lax.psum_scatter(totals, ("dp", "seq"), scatter_dimension=0, tiled=True)
    return (jnp.concatenate(outs_rows, 0), jnp.concatenate(outs_grads, 0)) + tuple(grads)


CORE, NEAR_X, NEAR_Y, ACROSS = 1, 2, 4, 6
GROUPS = 4


def tie(*values):
    return lax.optimization_barrier(values)


def swap(value, mask):
    return lax.ppermute(value, "seq", [(item, item ^ mask) for item in range(8)])


def pick(value, index, axis=0):
    return lax.dynamic_index_in_dim(value, index, axis, keepdims=False)


def in_order(own, other, bit, axis):
    return jnp.where(
        bit == 0, jnp.stack([own, other], axis), jnp.stack([other, own], axis)
    )


def plus(left, right):
    return (left.astype(jnp.float32) + right.astype(jnp.float32)).astype(jnp.bfloat16)


def total_of(parts):
    return sum(part.astype(jnp.float32) for part in parts)


def chips(value):
    return [value] + [swap(value, mask) for mask in (NEAR_X, NEAR_Y, ACROSS)]


def chips_send(order):
    got = [order(0)]
    for item, mask in ((1, NEAR_X), (2, NEAR_Y), (3, ACROSS)):
        got.append(swap(order(item), mask))
    return got


def chips_order(parts, chip):
    parts = jnp.stack(parts)
    return jnp.stack([pick(parts, chip ^ item) for item in range(GROUPS)])


def column_parts(value, count):
    parts = [value]
    for shift in range(1, count):
        perm = [(item, (item + shift) % count) for item in range(count)]
        parts.append(lax.ppermute(value, "dp", perm))
    return parts


def column_order(parts, place):
    count = len(parts)
    parts = jnp.stack(parts)
    return jnp.stack([pick(parts, (place - item) % count) for item in range(count)])


def column_send(value, place, count):
    parts = [pick(value, place)]
    for shift in range(1, count):
        sent = pick(value, (place + shift) % count)
        perm = [(item, (item + shift) % count) for item in range(count)]
        parts.append(lax.ppermute(sent, "dp", perm))
    return parts


def norm_parts(value):
    center = value - jnp.mean(value, -1, keepdims=True)
    spread_rows = jnp.mean(center * center, -1, keepdims=True)
    scale = lax.rsqrt(spread_rows + 1e-05)
    return center * scale, scale


def norm_back(normal, scale, gain, grad):
    through = grad * gain
    kept = through - jnp.mean(through, -1, keepdims=True)
    kept = kept - normal * jnp.mean(through * normal, -1, keepdims=True)
    return scale * kept


def dot(left, right):
    return jnp.dot(left, right, preferred_element_type=jnp.float32)


def dot_right(left, right):
    return lax.dot_general(
        left, right, (((1,), (1,)), ((), ())), preferred_element_type=jnp.float32
    )


def dot_left(left, right):
    return lax.dot_general(
        left, right, (((0,), (0,)), ((), ())), preferred_element_type=jnp.float32
    )


BLOCK = 256
VMEM_BYTES = 60 * 1024 * 1024


def head_mask(head, count):
    lane = lax.broadcasted_iota(jnp.int32, (1, count), 1)
    inside = (lane >= head * HEAD_DIM) & (lane < (head + 1) * HEAD_DIM)
    return inside.astype(jnp.float32).astype(jnp.bfloat16)


def head_rows(head):
    return pl.ds(pl.multiple_of(head * HEAD_DIM, HEAD_DIM), HEAD_DIM)


def flipped(value):
    return value.astype(jnp.float32).T.astype(jnp.bfloat16)


def attend_kernel(
    place_ref, own_ref, x_ref, y_ref, across_ref, w_near, w_far, vectors_ref, bias_ref, row_ref,
    normal_ref, normed_ref, w_ref, q_ref, k_ref, v_ref, full_ref, out_ref, p_ref,
    v_flip, held, column_ref,
):
    head = pl.program_id(0)
    length, count = q_ref.shape

    @pl.when(head == 0)
    def first():
        chip, core, column = place_ref[0] // 2, place_ref[0] % 2, place_ref[1]
        rows = out_ref.shape[2]
        for item, mine in enumerate((own_ref, x_ref, y_ref, across_ref)):
            for side in range(2):
                place = pl.ds(pl.multiple_of((2 * (chip ^ item) + side) * rows, rows), rows)
                normal, _ = norm_parts(mine[side, :rows].astype(jnp.float32))
                normal_ref[place] = normal.astype(jnp.bfloat16)
                normed = normal * vectors_ref[0:1] + vectors_ref[1:2]
                normed_ref[place] = normed.astype(jnp.bfloat16)
        columns, half, _ = w_near.shape
        for shift in range(columns):
            top = lax.rem(column - shift + columns, columns) * 2
            w_ref[pl.ds(pl.multiple_of((top + core) * half, 16), half)] = w_near[shift]
            w_ref[pl.ds(pl.multiple_of((top + 1 - core) * half, 16), half)] = w_far[shift]
        column_ref[...] = jnp.broadcast_to(row_ref[...], (128, length)).T
        for start in range(0, length, BLOCK):
            rows = pl.ds(start, BLOCK)
            product = dot(normed_ref[rows], w_ref[...]) + bias_ref[...]
            q_ref[rows] = (product[:, :count] * 0.125).astype(jnp.bfloat16)
            k_ref[rows] = product[:, count : 2 * count].astype(jnp.bfloat16)
            v_ref[rows] = product[:, 2 * count :].astype(jnp.bfloat16)
        v_flip[...] = flipped(v_ref[...])

    mask = head_mask(head, count)
    for start in range(0, length, BLOCK):
        stop = start + BLOCK
        scores = dot_right(k_ref[:stop], q_ref[start:stop] * mask)
        shape = (stop, BLOCK)
        causal = lax.broadcasted_iota(jnp.int32, shape, 0) <= start + lax.broadcasted_iota(
            jnp.int32, shape, 1
        )
        same = column_ref[:stop, 0:1] == row_ref[:, start:stop]
        scores = jnp.where(causal & same, scores, -1000000000.0)
        expo = jnp.exp(scores - jnp.max(scores, 0, keepdims=True))
        probs = (expo * (1.0 / jnp.sum(expo, 0, keepdims=True))).astype(jnp.bfloat16)
        p_ref[0, :stop, start:stop] = probs
        held[head_rows(head), start:stop] = dot(v_flip[head_rows(head), :stop], probs)

    @pl.when(head == pl.num_programs(0) - 1)
    def last():
        full_ref[...] = held[...]
        blocks, _, rows = out_ref.shape
        for block in range(blocks):
            out_ref[block] = held[:, block * rows : (block + 1) * rows].astype(jnp.bfloat16)


def attend_back_kernel(
    chip_ref, q_ref, k_ref, v_ref, d_ref, full_ref, normed_ref, w_ref, normal_ref, terms_in, p_ref,
    near_ref, far_ref, first_0, first_1, first_2, first_3, terms_ref,
    k_flip, dots, dq, dk, dv, d_all, d_held, grad,
):
    head = pl.program_id(0)
    length, count = q_ref.shape

    @pl.when(head == 0)
    def first():
        k_flip[...] = flipped(k_ref[...])
        blocks, _, rows = d_ref.shape
        for block in range(blocks):
            place = pl.ds(block * rows, rows)
            d_out = d_ref[block].astype(jnp.float32)
            d_held[place] = d_out.T.astype(jnp.bfloat16)
            dots[:, place] = d_out * full_ref[:, place]
        dk[...] = jnp.zeros_like(dk)
        dv[...] = jnp.zeros_like(dv)

    mask = head_mask(head, count)
    for start in range(0, length, BLOCK):
        stop = start + BLOCK
        d_out = d_held[start:stop] * mask
        probs = p_ref[0, :stop, start:stop]
        row_dots = jnp.sum(dots[head_rows(head), start:stop], 0, keepdims=True)
        d_probs = dot_right(v_ref[:stop], d_out)
        d_scores = (probs.astype(jnp.float32) * (d_probs - row_dots)).astype(jnp.bfloat16)
        dv[:stop] += dot(probs, d_out)
        dk[:stop] += dot(d_scores, q_ref[start:stop] * mask)
        dq[head_rows(head), start:stop] = dot(k_flip[head_rows(head), :stop], d_scores)

    @pl.when(head == pl.num_programs(0) - 1)
    def last():
        for start in range(0, length, BLOCK):
            rows = pl.ds(start, BLOCK)
            d_queries = dq[:, start : start + BLOCK].T.astype(jnp.bfloat16).astype(jnp.float32)
            d_all[rows] = jnp.concatenate([d_queries * 0.125, dk[rows], dv[rows]], 1).astype(
                jnp.bfloat16
            )
        width = normed_ref.shape[1]
        lane = lax.broadcasted_iota(jnp.int32, (1, width), 1) - chip_ref[0] * count
        inside = ((lane >= 0) & (lane < count)).astype(jnp.float32)
        bias = jnp.sum(d_all[...].astype(jnp.float32), 0, keepdims=True)
        bias = [
            jnp.concatenate([bias[:, item * count : (item + 1) * count]] * GROUPS, 1) * inside
            for item in (0, 2)
        ]
        grad[...] = dot_left(normed_ref[...], d_all[...])
        columns, half, _ = near_ref.shape
        for column in range(columns):
            for order, part_ref in enumerate((near_ref, far_ref)):
                start = pl.multiple_of((2 * column + (chip_ref[1] ^ order)) * half, half)
                part_ref[column] = grad[pl.ds(start, half)].astype(jnp.bfloat16)
        gain = shift = jnp.zeros((1, width), jnp.float32)
        for item in range(GROUPS):
            size = length // GROUPS
            rows = pl.ds(pl.multiple_of((chip_ref[0] ^ item) * size, size), size)
            d_first = dot_right(d_all[rows], w_ref[...])
            gain += jnp.sum(d_first * normal_ref[rows].astype(jnp.float32), 0, keepdims=True)
            shift += jnp.sum(d_first, 0, keepdims=True)
            (first_0, first_1, first_2, first_3)[item][...] = d_first.astype(jnp.bfloat16)
        row = lax.broadcasted_iota(jnp.int32, (16, 1), 0)
        terms = terms_in[...]
        for item, value in ((0, bias[0]), (1, bias[1]), (4, gain), (5, shift)):
            terms = jnp.where(row == item, value, terms)
        coarse = terms.astype(jnp.bfloat16).astype(jnp.float32)
        fine = terms - coarse
        columns = terms_ref.shape[0]
        size = width // columns
        for column in range(columns):
            part = slice(column * size, (column + 1) * size)
            terms_ref[column] = jnp.concatenate(
                [coarse[:, part], fine[:, part], jnp.zeros((16, count * 3 - 2 * size), jnp.float32)], 1
            ).astype(jnp.bfloat16)


def whole(*shape):
    return pl.BlockSpec(shape, lambda head: (0,) * len(shape))


def kernel_params():
    return pltpu.CompilerParams(
        dimension_semantics=("arbitrary",), vmem_limit_bytes=VMEM_BYTES
    )


def attend(place, column, mine, near, far, vectors, bias, segments):
    _, padded, width = mine[0].shape
    columns, half, _ = near.shape
    length = segments.shape[0]
    count = near.shape[2] // 3
    heads = count // HEAD_DIM
    shape = (length, count)
    blocks = (2 * GROUPS, count, length // (2 * GROUPS))
    probs = pl.BlockSpec((1, length, length), lambda head: (head, 0, 0))
    normal, normed, weights, queries, keys, values, full, out, probs = pl.pallas_call(
        attend_kernel,
        grid=(heads,),
        in_specs=[pl.BlockSpec(memory_space=pltpu.SMEM)]
        + [whole(2, padded, width)] * 4
        + [whole(*near.shape)] * 2
        + [whole(8, width), whole(1, 3 * count), whole(1, length)],
        out_specs=[whole(length, width)] * 2
        + [whole(width, 3 * count)]
        + [whole(*shape)] * 3
        + [whole(count, length), whole(*blocks), probs],
        out_shape=[
            low(length, width),
            low(length, width),
            low(width, 3 * count),
            low(*shape),
            low(*shape),
            low(*shape),
            one(count, length),
            low(*blocks),
            low(heads, length, length),
        ],
        scratch_shapes=[
            pltpu.VMEM((count, length), jnp.bfloat16),
            pltpu.VMEM((count, length), jnp.float32),
            pltpu.VMEM((length, 128), jnp.float32),
        ],
        compiler_params=kernel_params(),
        cost_estimate=pl.CostEstimate(
            flops=4 * length * length * count + 6 * length * width * count,
            bytes_accessed=2 * heads * length * length,
            transcendentals=heads * length * length,
        ),
    )(jnp.stack([place, column]), *mine, near, far, vectors, bias[None], segments[None])
    return out, (queries, keys, values), (full, probs), (normal, normed, weights)


def attend_back(place, columns, projected, kept, d_out, normed, weights, normal, terms):
    length, width = normed.shape
    count = d_out.shape[1]
    heads = count // HEAD_DIM
    shape = (length, count)
    full, probs = kept
    size = length // GROUPS
    return pl.pallas_call(
        attend_back_kernel,
        grid=(heads,),
        in_specs=[pl.BlockSpec(memory_space=pltpu.SMEM)]
        + [whole(*shape)] * 3
        + [
            whole(*d_out.shape),
            whole(count, length),
            whole(length, width),
            whole(width, 3 * count),
            whole(length, width),
            whole(16, width),
            pl.BlockSpec((1, length, length), lambda head: (head, 0, 0)),
        ],
        out_specs=[
            whole(columns, width // columns // 2, 3 * count),
            whole(columns, width // columns // 2, 3 * count),
            whole(size, width),
            whole(size, width),
            whole(size, width),
            whole(size, width),
            whole(columns, 16, 3 * count),
        ],
        out_shape=[
            low(columns, width // columns // 2, 3 * count),
            low(columns, width // columns // 2, 3 * count),
            low(size, width),
            low(size, width),
            low(size, width),
            low(size, width),
            low(columns, 16, 3 * count),
        ],
        scratch_shapes=[
            pltpu.VMEM((count, length), jnp.bfloat16),
            pltpu.VMEM((count, length), jnp.float32),
            pltpu.VMEM((count, length), jnp.float32),
            pltpu.VMEM(shape, jnp.float32),
            pltpu.VMEM(shape, jnp.float32),
            pltpu.VMEM((length, 3 * count), jnp.bfloat16),
            pltpu.VMEM(shape, jnp.bfloat16),
            pltpu.VMEM((width, 3 * count), jnp.float32),
        ],
        compiler_params=kernel_params(),
        cost_estimate=pl.CostEstimate(
            flops=10 * length * length * count + 12 * length * width * count,
            bytes_accessed=2 * heads * length * length,
            transcendentals=0,
        ),
    )(jnp.stack([place // 2, place % 2]), *projected, d_out, full, normed, weights, normal, terms, probs)


def one(*shape):
    return jax.ShapeDtypeStruct(shape, jnp.float32)


def low(*shape):
    return jax.ShapeDtypeStruct(shape, jnp.bfloat16)


def run(body, given, outs, flops, scratch=(), scalars=()):
    specs = [pl.BlockSpec(memory_space=pltpu.SMEM)] * len(scalars)
    return pl.pallas_call(
        body,
        grid=(1,),
        in_specs=specs + [whole(*item.shape) for item in given],
        out_specs=[whole(*item.shape) for item in outs],
        out_shape=list(outs),
        scratch_shapes=list(scratch),
        compiler_params=pltpu.CompilerParams(vmem_limit_bytes=VMEM_BYTES),
        cost_estimate=pl.CostEstimate(flops=flops, bytes_accessed=0, transcendentals=0),
    )(*[item[None] for item in scalars], *given)


def second_kernel(attended_ref, w_ref, in_ref, vectors_ref, middle_ref, second_ref):
    blocks, count, rows = attended_ref.shape
    groups, seqs = blocks // 2, 2
    for seq in range(seqs):
        place = pl.ds(seq * rows, rows)
        middle = in_ref[place].astype(jnp.float32) + vectors_ref[0:1]
        for group in range(groups):
            middle += dot_left(
                attended_ref[seqs * group + seq], w_ref[group * count : (group + 1) * count]
            )
        middle_ref[place] = middle
        normal, _ = norm_parts(middle)
        second_ref[place] = (normal * vectors_ref[1:2] + vectors_ref[2:3]).astype(jnp.bfloat16)


def branch_kernel(
    place_ref, own_ref, x_ref, y_ref, across_ref, grad_ref, middle_ref, vectors_ref, w_ref,
    attended_ref, bias_ref, d_middle_ref, d_attended_ref, sums_ref, near_ref, far_ref, total,
):
    blocks, count, rows = d_attended_ref.shape
    groups, seqs = blocks // 2, 2
    d_second = total_of([own_ref[...], x_ref[...], y_ref[...], across_ref[...]])
    normal, scale = norm_parts(middle_ref[...])
    d_middle = grad_ref[...].astype(jnp.float32) + norm_back(
        normal, scale, vectors_ref[1:2], d_second
    )
    d_middle_ref[...] = d_middle
    d_branch = d_middle.astype(jnp.bfloat16)
    for group in range(groups):
        part = dot_right(w_ref[group * count : (group + 1) * count], d_branch)
        part = part.astype(jnp.bfloat16)
        for seq in range(seqs):
            d_attended_ref[seqs * group + seq] = part[:, seq * rows : (seq + 1) * rows]
        total[group * count : (group + 1) * count] = sum(
            dot(attended_ref[seqs * group + seq], d_branch[seq * rows : (seq + 1) * rows])
            for seq in range(seqs)
        )
    chips_count, columns, share, _ = near_ref.shape
    for order, grad_out_ref in enumerate((near_ref, far_ref)):
        for item in range(chips_count):
            owner = place_ref[0] ^ (2 * item + order)
            for column in range(columns):
                start = pl.multiple_of((column * blocks + owner) * share, 8)
                grad_out_ref[item, column] = total[pl.ds(start, share)].astype(jnp.bfloat16)
    sums_ref[...] = jnp.zeros_like(sums_ref)
    sums_ref[2:3] = jnp.sum(d_branch.astype(jnp.float32), 0, keepdims=True)
    sums_ref[3:4] = jnp.sum(grad_ref[...].astype(jnp.float32), 0, keepdims=True)
    sums_ref[6:7] = jnp.sum(d_second * normal, 0, keepdims=True)
    sums_ref[7:8] = jnp.sum(d_second, 0, keepdims=True)
    sums_ref[8:12] = bias_ref[...]


def hidden_kernel(*refs):
    count = (len(refs) - 4) // 5
    groups = [refs[count * item : count * (item + 1)] for item in range(2)]
    w_up, w_down, bias_ref = refs[2 * count : 2 * count + 3]
    groups += [refs[count * item + 3 : count * (item + 1) + 3] for item in range(2, 5)]
    sums_ref = refs[-1]
    slope = 0.7978845608028654
    sums_ref[...] = jnp.zeros_like(sums_ref)
    for row_ref, grad_ref, act_ref, d_upper_ref, d_rows_ref in zip(*groups):
        upper = dot(row_ref[...], w_up[...]) + bias_ref[...]
        square = upper * upper
        bend = jnp.tanh(slope * (upper + 0.044715 * (square * upper)))
        act_ref[...] = (0.5 * upper * (1.0 + bend)).astype(jnp.bfloat16)
        rise = 0.5 * (1.0 + bend) + (0.5 * slope) * upper * (1.0 - bend * bend) * (
            1.0 + (3.0 * 0.044715) * square
        )
        d_upper = (dot_right(grad_ref[...], w_down[...]) * rise).astype(jnp.bfloat16)
        d_upper_ref[...] = d_upper
        sums_ref[0:1] += jnp.sum(d_upper.astype(jnp.float32), 0, keepdims=True)
        d_rows_ref[...] = dot_right(d_upper, w_up[...]).astype(jnp.bfloat16)


def hidden_weights_kernel(core_ref, *refs):
    groups = [refs[4 * item : 4 * item + 4] for item in range(4)]
    w_down, *down_refs, late_near, late_far, up, down = refs[16:]
    for item, (row_ref, grad_ref, act_ref, d_upper_ref) in enumerate(zip(*groups)):
        down_refs[item][...] = dot(act_ref[...], w_down[...]).astype(jnp.bfloat16)
        up_term = dot_left(row_ref[...], d_upper_ref[...])
        down_term = dot_left(act_ref[...], grad_ref[...])
        if item == 0:
            up[...] = up_term
            down[...] = down_term
        else:
            up[...] += up_term
            down[...] += down_term
    columns, both, width = late_near.shape
    half, side = both // 2, width // 2
    for order in range(2):
        late_ref = (late_near, late_far)[order]
        start = pl.multiple_of((core_ref[0] ^ order) * side, side)
        for column in range(columns):
            top = column * both
            for part in range(2):
                late_ref[column, :half, part * side : (part + 1) * side] = up[
                    top + part * half : top + (part + 1) * half, pl.ds(start, side)
                ].astype(jnp.bfloat16)
            late_ref[column, half:] = down[
                pl.ds(pl.multiple_of(start + column * half, 8), half)
            ].astype(jnp.bfloat16)


def plane_local(
    hidden_in,
    cotangent,
    segment_ids,
    query_weight,
    key_weight,
    value_weight,
    out_weight,
    up_weight,
    down_weight,
    query_bias,
    value_bias,
    out_bias,
    up_bias,
    down_bias,
    first_gain,
    first_shift,
    second_gain,
    second_shift,
):
    seqs, rows, width = hidden_in.shape
    plane = lax.axis_size("seq")
    columns = lax.axis_size("dp")
    owners = plane * columns
    share = query_weight.shape[0]
    ff_share = down_weight.shape[0]
    hidden = up_weight.shape[1]
    group_width = width // GROUPS
    length = rows * plane
    tokens = seqs * rows
    half = plane * share // 2
    column = lax.axis_index("dp")
    place = lax.axis_index("seq")
    core, chip = place % 2, place // 2

    sent = jnp.stack([query_weight, key_weight, value_weight], 1)
    sent = sent.reshape(share, 3, GROUPS, group_width).transpose(2, 0, 1, 3)
    sent = jnp.repeat(sent.reshape(GROUPS, share, 3 * group_width), 2, axis=0)
    sent_up = up_weight.reshape(share, columns, plane, ff_share).transpose(2, 0, 1, 3)
    sent_up = sent_up.reshape(plane, share, columns * ff_share)
    sent = jnp.concatenate([sent, sent_up], -1)

    small = (
        query_bias,
        value_bias,
        out_bias,
        down_bias,
        first_gain,
        first_shift,
        second_gain,
        second_shift,
        up_bias,
        segment_ids,
    )
    sent, small, out_weight = tie(sent, small, out_weight)
    got = lax.all_to_all(sent, "seq", 0, 0, tiled=True).reshape(plane * share, -1)
    small = jnp.concatenate(small[:-1] + (small[-1].astype(jnp.bfloat16).reshape(-1),))
    small_size = small.size
    small = jnp.pad(small[None], ((0, 7), (0, width - small_size)))
    small = column_parts(jnp.concatenate([out_weight, small]), columns)
    mine = in_order(pick(hidden_in, core), swap(pick(hidden_in, 1 - core), CORE), core, 0)
    beside = chips(cotangent.reshape(tokens, width))
    got, small, mine, beside = tie(got, small, mine, beside)

    got_up = got[:, 3 * group_width :]
    w_qkv = pick(got[:, : 3 * group_width].reshape(2, half, -1), core)
    w_qkv = column_parts(w_qkv, columns)
    later = jnp.concatenate([got_up[:half], got_up[half:], down_weight], -1)
    later = jnp.broadcast_to(later, (columns,) + later.shape)
    later = lax.all_to_all(later, "dp", 0, 0, tiled=True)

    small = column_order(small, column)
    w_out = small[:, :share].reshape(columns * share, width)
    small = jnp.pad(small[:, share], ((0, -columns % 8), (0, 0)))
    small = in_order(small, swap(small, CORE), core, 0)
    mine = chips(jnp.concatenate([mine, small], 1))
    small = chips_order([item[:, rows : rows + columns] for item in mine], chip)
    small = small.reshape(plane, columns, width).transpose(1, 0, 2)
    vectors = small[:, :, : 8 * share].astype(jnp.float32).reshape(owners, 8, share)
    vectors = vectors.transpose(1, 0, 2).reshape(8, width)
    bq, bv, bo, bd, gain_one, shift_one, gain_two, shift_two = [vectors[i] for i in range(8)]
    bu = small[:, :, 8 * share : 8 * share + ff_share].astype(jnp.float32)
    bu = pick(bu.reshape(columns, GROUPS, 2, ff_share), chip, 1).transpose(1, 0, 2).reshape(-1)
    segments = pick(small[:, :, 8 * share + ff_share : small_size], column)
    segments = pick(segments.reshape(plane, seqs, rows), core, 1).reshape(length)
    segments = segments.astype(jnp.float32)
    first_vectors = jnp.stack([gain_one, shift_one] + [jnp.zeros_like(bo)] * 6)
    own_columns = lambda item: lax.dynamic_slice_in_dim(item, chip * group_width, group_width)
    bias_here = jnp.concatenate([own_columns(bq), jnp.zeros((group_width,)), own_columns(bv)])

    w_out = in_order(w_out, swap(w_out, CORE), core, 0)
    mine, w_out = tie(mine, w_out)
    w_out = chips(w_out)
    first_vectors, bias_here, segments, w_qkv = tie(first_vectors, bias_here, segments, w_qkv)
    w_qkv = jnp.stack(w_qkv)
    attended, projected, kept, (normal_all, normed, w_qkv) = attend(
        place, column, mine, w_qkv, swap(w_qkv, CORE), first_vectors, bias_here, segments
    )
    attended, beside, later, w_out = tie(attended, beside, later, w_out)
    later_far = swap(later, CORE)
    w_out = chips_order(w_out, chip).reshape(plane, columns, share, width)
    w_out = w_out.transpose(1, 0, 2, 3).reshape(width, width)
    attended = lax.all_to_all(attended, "seq", 0, 0, tiled=True)
    block_in = hidden_in.reshape(tokens, width)
    norm_vectors = jnp.stack([bo, gain_two, shift_two] + [jnp.zeros_like(bo)] * 5)
    middle, second = run(
        second_kernel,
        (attended, w_out, block_in, norm_vectors),
        (one(tokens, width), low(tokens, width)),
        2 * tokens * width * width,
    )
    second = chips(second)
    later = in_order(later, later_far, core, 0)
    w_down = later[..., width:].reshape(width, width)
    w_up = jnp.concatenate(
        [
            later[item, ..., width // 2 * side : width // 2 * (side + 1)]
            for side in range(2)
            for item in range(2)
        ],
        -1,
    )
    w_up = w_up.reshape(columns, half, 2, width).transpose(0, 2, 1, 3).reshape(width, width)

    acts, d_uppers, d_rows, d_bu = [], [], [], 0.0
    for part in (slice(0, 1), slice(1, 4)):
        count = len(second[part])
        *outs, sums = run(
            hidden_kernel,
            (*second[part], *beside[part], w_up, w_down, bu[None]),
            (*[low(tokens, width)] * (3 * count), one(8, width)),
            12 * count * tokens * width * width,
        )
        acts += outs[:count]
        d_uppers += outs[count : 2 * count]
        d_rows += outs[2 * count :]
        d_bu = d_bu + sums
    d_second = [swap(d_rows[i], mask) for i, mask in ((1, NEAR_X), (2, NEAR_Y), (3, ACROSS))]
    acts, d_rows = tie(acts, d_rows)
    *down, late, late_far = run(
        hidden_weights_kernel,
        (*second, *beside, *acts, *d_uppers, w_down),
        (*[low(tokens, width)] * 4, *[low(columns, 2 * half, width)] * 2),
        24 * tokens * width * width,
        [pltpu.VMEM((width, width), jnp.float32)] * 2,
        (core,),
    )
    d_second, late, late_far, down = tie(d_second, late, late_far, down)
    late = plus(late, swap(late_far, CORE))
    d_bu = lax.dynamic_update_slice_in_dim(
        jnp.zeros((columns, GROUPS, 2, ff_share), jnp.float32),
        d_bu[0].reshape(2, columns, 1, ff_share).transpose(1, 2, 0, 3),
        chip,
        1,
    )
    d_bu = d_bu.reshape(owners, -1, share).transpose(1, 0, 2).reshape(-1, width)
    d_middle, d_attended, terms, grad_out, grad_far = run(
        branch_kernel,
        (
            d_rows[0],
            *d_second,
            cotangent.reshape(tokens, width),
            middle,
            norm_vectors,
            w_out,
            attended,
            d_bu,
        ),
        (
            one(tokens, width),
            low(plane, group_width, rows),
            one(16, width),
            *[low(GROUPS, columns, share, width)] * 2,
        ),
        4 * tokens * width * width,
        [pltpu.VMEM((width, width), jnp.float32)],
        (place,),
    )
    late = column_send(late, column, columns)
    d_attended = lax.all_to_all(d_attended, "seq", 0, 0, tiled=True)
    grad_out = plus(grad_out, swap(grad_far, CORE))
    d_attended, down, late[1] = tie(d_attended, down, late[1])
    grad_out = [grad_out[0]] + [
        swap(grad_out[i], mask) for i, mask in ((1, NEAR_X), (2, NEAR_Y), (3, ACROSS))
    ]
    down = [down[0]] + [
        swap(down[i], mask) for i, mask in ((1, NEAR_X), (2, NEAR_Y), (3, ACROSS))
    ]
    grad_near, grad_far, *d_first, terms = attend_back(
        place, columns, projected, kept, d_attended, normed, w_qkv, normal_all, terms
    )
    grad_near, grad_far, terms, grad_out, down, late = tie(
        grad_near, grad_far, terms, grad_out, down, late
    )

    grad_qkv = plus(grad_near, swap(grad_far, CORE))
    grad_out = total_of(grad_out).astype(jnp.bfloat16).reshape(columns, -1, 3 * group_width)
    last = jnp.concatenate([grad_qkv, grad_out, terms], 1)
    last = lax.all_to_all(last, "dp", 0, 0, tiled=True)
    d_first = [d_first[0]] + [
        swap(d_first[item], mask) for item, mask in ((1, NEAR_X), (2, NEAR_Y), (3, ACROSS))
    ]

    last, late = tie(last, late)
    last, late = jnp.sum(last.astype(jnp.float32), 0), total_of(late)
    grad_up = jnp.concatenate([late[:half, : width // 2], late[:half, width // 2 :]])
    grad_down = late[half:]
    grad_out = last[half:-16].reshape(share, width)
    terms = last[-16:, :group_width] + last[-16:, group_width : 2 * group_width]
    terms = terms[:12].T
    last = last[:half].astype(jnp.bfloat16)
    last = in_order(last, swap(last, CORE), core, 0).reshape(plane * share, -1)
    coarse = lax.reduce_precision(terms, 8, 7)
    terms = jnp.concatenate([coarse, terms - coarse], -1)
    last = jnp.concatenate([last, terms.astype(jnp.bfloat16), grad_up.astype(jnp.bfloat16)], -1)
    last = lax.all_to_all(last.reshape(plane, share, -1), "seq", 0, 0, tiled=True)
    last = last.astype(jnp.float32)
    grad_up = last[..., -columns * ff_share :].reshape(plane, share, columns, ff_share)
    grad_up = grad_up.transpose(1, 2, 0, 3).reshape(share, hidden)
    terms = jnp.sum(last[..., 3 * group_width : -columns * ff_share], 0)
    terms = terms[:, : terms.shape[1] // 2] + terms[:, terms.shape[1] // 2 :]
    terms = terms.T
    g_bu = terms[8:].reshape(-1)
    g_bq, g_bv, g_bo, g_bd, g_g1, g_s1, g_g2, g_s2 = [terms[i] for i in range(8)]
    grad_qkv = last[::2, :, : 3 * group_width].reshape(GROUPS, share, 3, group_width)
    grad_qkv = grad_qkv.transpose(2, 1, 0, 3).reshape(3, share, width)

    d_first = total_of(d_first).astype(jnp.bfloat16).reshape(2, rows, width)
    d_first = in_order(pick(d_first, core), swap(pick(d_first, 1 - core), CORE), core, 0)
    d_first = d_first.reshape(tokens, width).astype(jnp.float32)
    normal_one, scale_one = norm_parts(block_in.astype(jnp.float32))
    grad_input = d_middle + norm_back(normal_one, scale_one, gain_one, d_first)
    hidden_out = (middle + total_of(down) + bd).astype(jnp.bfloat16)
    return (
        hidden_out.reshape(seqs, rows, width),
        grad_input.reshape(seqs, rows, width),
        grad_qkv[0],
        grad_qkv[1],
        grad_qkv[2],
        grad_out,
        grad_up,
        grad_down,
        g_bq,
        g_bv,
        g_bo,
        g_bu,
        g_bd,
        g_g1,
        g_s1,
        g_g2,
        g_s2,
    )


def solution(mesh):
    plane = mesh.shape["seq"] == 8 and HEADS % 4 == 0
    body = plane_local if plane else wide_local
    placed = (
        P("dp", "seq", None),
        P("dp", "seq", None),
        P("dp", "seq"),
        P(("dp", "seq"), None),
        P(("dp", "seq"), None),
        P(("dp", "seq"), None),
        P(("dp", "seq"), None),
        P(("dp", "seq"), None),
        P(("dp", "seq"), None),
        P(("dp", "seq")),
        P(("dp", "seq")),
        P(("dp", "seq")),
        P(("dp", "seq")),
        P(("dp", "seq")),
        P(("dp", "seq")),
        P(("dp", "seq")),
        P(("dp", "seq")),
        P(("dp", "seq")),
    )
    return jax.shard_map(
        body,
        mesh=mesh,
        in_specs=placed,
        out_specs=(
            P("dp", "seq", None),
            P("dp", "seq", None),
            P(("dp", "seq"), None),
            P(("dp", "seq"), None),
            P(("dp", "seq"), None),
            P(("dp", "seq"), None),
            P(("dp", "seq"), None),
            P(("dp", "seq"), None),
            P(("dp", "seq")),
            P(("dp", "seq")),
            P(("dp", "seq")),
            P(("dp", "seq")),
            P(("dp", "seq")),
            P(("dp", "seq")),
            P(("dp", "seq")),
            P(("dp", "seq")),
            P(("dp", "seq")),
        ),
        check_vma=False,
    )
```
